128 devices in a mesh: chan: 4 (over x_hi, core), pulse: 32 (over x_lo, y, z).
Axes of the slice: x: 4 (x_hi: 2, x_lo: 2; x = x_hi * 2 + x_lo), y: 4, z: 4, core: 2. Of those that a mesh axis runs over, the one named last changes fastest.
Arguments:
- echo_re: bfloat16 [8, 4096, 8192], P('chan', 'pulse'), may hold values from -6 to 6
- echo_im: bfloat16 [8, 4096, 8192], P('chan', 'pulse'), may hold values from -6 to 6
- range_filter_re: float32 [8192], replicated, may hold values from -6 to 6
- range_filter_im: float32 [8192], replicated, may hold values from -6 to 6
- beam_weight_re: float32 [8, 8192], P('chan'), may hold values from -3 to 3
- beam_weight_im: float32 [8, 8192], P('chan'), may hold values from -3 to 3
- window_start: int32 [64], replicated, may hold values from 0 to 4
- azimuth_filter_re: float32 [8192, 4096], P(('chan', 'pulse')), may hold values from -6 to 6
- azimuth_filter_im: float32 [8192, 4096], P(('chan', 'pulse')), may hold values from -6 to 6
- migration_rate: float32 [8192], P(('chan', 'pulse')), may hold values from 0.5 to 8
Outputs:
- image_re: float32 [8192, 4096], P(('chan', 'pulse'))
- image_im: float32 [8192, 4096], P(('chan', 'pulse'))
The draws below stay inside these ranges and needn't reach their ends.
Inputs may be any that keep to these rules, and one draw needn't show every extreme that they name: window_start of a range block is the first of the 4 consecutive channels that receive its echo.
All inputs are finite; a program needn't handle non-finite values.
Results may differ from the reference program's by a relative error of at most 0.0085.
Values may be sent and summed in bfloat16 or wider, within the bound.
A program may use at most 128 MiB of HBM per device.

```python
import math
import jax
import jax.numpy as jnp
from jax import lax

CH = 8
ACTIVE = 4
R = 8192
NB = 64
P_SIZE = 4096
N_CHAN = 4


def plant(array, own_key, smallest, largest):
    longest = array.shape.index(max(array.shape))
    spots = []
    for shift in (0, 1):
        where = [jax.random.randint(jax.random.fold_in(own_key, axis), (), 0, length) for axis, length in enumerate(array.shape)]
        where[longest] = (where[longest] + shift) % array.shape[longest]
        spots.append(tuple(where))
    return array.at[spots[0]].set(smallest).at[spots[1]].set(largest)


def steps_of(own_key, extent, pieces, low, top_value):
    def one(dim, blocks):
        heights = jax.random.uniform(jax.random.fold_in(jax.random.fold_in(own_key, 6), dim), (blocks,), jnp.float32, low / len(pieces), top_value / len(pieces))
        return jnp.repeat(jnp.exp(heights), extent[dim] // blocks).reshape((-1,) + (1,) * (len(extent) - dim - 1))

    loudness = one(*pieces[0])
    for cut in pieces[1:]:
        loudness = loudness * one(*cut)
    return loudness


def bell_draw(own_key, shape, scale, reach, shards=(), kind=jnp.bfloat16):
    array = scale * jax.random.normal(own_key, shape, jnp.float32)
    if shards:
        array = array * steps_of(own_key, shape, shards, -0.22, 0.18)
    return jnp.clip(array, -reach, reach).astype(kind)


def setup_inputs(seed: int = 0) -> dict:
    splits = jax.random.split(jax.random.key(seed), 11)
    echo_re = bell_draw(splits[0], (CH, P_SIZE, R), 1.0, 6.0, ((0, 4), (1, 32)))
    echo_im = bell_draw(splits[1], (CH, P_SIZE, R), 1.0, 6.0, ((0, 4), (1, 32)))
    range_filter_re = bell_draw(splits[2], (R,), 1.0, 6.0, (), jnp.float32)
    range_filter_im = bell_draw(splits[3], (R,), 1.0, 6.0, (), jnp.float32)
    beam_weight_re = bell_draw(splits[4], (CH, R), 0.5, 3.0, ((0, 4),), jnp.float32)
    beam_weight_im = bell_draw(splits[5], (CH, R), 0.5, 3.0, ((0, 4),), jnp.float32)
    window_start = plant(jax.random.randint(splits[6], (NB,), 0, CH - ACTIVE + 1), jax.random.fold_in(splits[6], 1), 0, CH - ACTIVE).astype(jnp.int32)
    azimuth_filter_re = bell_draw(splits[7], (R, P_SIZE), 1.0, 6.0, ((0, 128),), jnp.float32)
    azimuth_filter_im = bell_draw(splits[8], (R, P_SIZE), 1.0, 6.0, ((0, 128),), jnp.float32)
    migration_rate = jnp.clip(jnp.exp(math.log(8.0) - 2.7725887 * jax.random.uniform(splits[9], (R,), jnp.float32) ** steps_of(splits[9], (R,), ((0, 128),), -0.2, 0.2)), 0.5, 8.0)
    return dict(echo_re=echo_re, echo_im=echo_im, range_filter_re=range_filter_re, range_filter_im=range_filter_im, beam_weight_re=beam_weight_re, beam_weight_im=beam_weight_im, window_start=window_start, azimuth_filter_re=azimuth_filter_re, azimuth_filter_im=azimuth_filter_im, migration_rate=migration_rate)


def compress_one(row_re, row_im, spectrum_filter, weight_row):
    signal = lax.complex(row_re.astype(jnp.float32), row_im.astype(jnp.float32))
    spectrum = jnp.fft.fft(signal, axis=-1)
    return jnp.fft.ifft(spectrum * spectrum_filter[None, :], axis=-1) * weight_row[None, :]


def reference(echo_re, echo_im, range_filter_re, range_filter_im, beam_weight_re, beam_weight_im, window_start, azimuth_filter_re, azimuth_filter_im, migration_rate):
    spectrum_filter = lax.complex(range_filter_re, range_filter_im)
    starts = jnp.repeat(window_start, R // NB)
    channel = jnp.arange(CH, dtype=jnp.int32)[:, None]
    active = ((channel >= starts[None, :]) & (channel < starts[None, :] + ACTIVE)).astype(jnp.float32)
    weights = lax.complex(beam_weight_re * active, beam_weight_im * active)
    per_group = CH // N_CHAN
    beam_re = jnp.zeros((P_SIZE, R), jnp.float32)
    beam_im = jnp.zeros((P_SIZE, R), jnp.float32)
    for group in range(N_CHAN):
        def single(channel_id):
            return compress_one(echo_re[channel_id], echo_im[channel_id], spectrum_filter, weights[channel_id])

        channel_ids = jnp.arange(group * per_group, (group + 1) * per_group, dtype=jnp.int32)
        summed = jnp.sum(lax.map(single, channel_ids), axis=0)
        rounded_re = lax.optimization_barrier(jnp.real(summed).astype(jnp.bfloat16))
        rounded_im = lax.optimization_barrier(jnp.imag(summed).astype(jnp.bfloat16))
        beam_re = beam_re + rounded_re.astype(jnp.float32)
        beam_im = beam_im + rounded_im.astype(jnp.float32)
    beam = lax.complex(beam_re, beam_im).T
    spectrum_az = jnp.fft.fft(beam, axis=-1)
    doppler = ((jnp.arange(P_SIZE, dtype=jnp.int32) + P_SIZE // 2) % P_SIZE - P_SIZE // 2).astype(jnp.float32) * (2.0 / P_SIZE)
    phase = math.pi * migration_rate[:, None] * doppler[None, :] ** 2
    factor = lax.complex(jnp.cos(phase), -jnp.sin(phase)) * lax.complex(azimuth_filter_re, azimuth_filter_im)
    image = jnp.fft.ifft(spectrum_az * factor, axis=-1)
    return jnp.real(image).astype(jnp.float32), jnp.imag(image).astype(jnp.float32)
```

```python
import functools
import math

import jax
import jax.numpy as jnp
import numpy as np
from jax import lax
from jax.experimental import pallas as pl
from jax.experimental.pallas import tpu as pltpu
from jax.sharding import PartitionSpec as P

ACTIVE = 4
F32 = jnp.float32
BF16 = jnp.bfloat16
MESH = pl.DeviceIdType.MESH
VMEM = pltpu.VMEM
MIB = 1024 * 1024

OUTER = 64
LANES = 128
RANGE = OUTER * LANES
AZ_OUTER = 32
PULSES = AZ_OUTER * LANES


def unit(numerator, denominator):
    angle = 2.0 * np.pi * (np.asarray(numerator) % denominator) / denominator
    return np.cos(angle), np.sin(angle)


def f32_pair(pair):
    return tuple(np.asarray(part, np.float32) for part in pair)


def range_tables():
    row = np.arange(OUTER)[:, None]
    lane = np.arange(LANES)[None, :]
    tables = []
    for parity in (0, 1):
        re, im = unit(lane * (2 * row + parity), LANES)
        tables += f32_pair((re / RANGE, im / RANGE))
    tables += f32_pair(unit(row * lane, RANGE))
    tables += f32_pair(unit(row * (lane - LANES), RANGE))
    return np.stack(tables)


def real_form(pair):
    re, im = pair
    return np.block([[re, im], [-im, re]])


def split_table(table):
    high = table.astype(BF16)
    low = (table - high.astype(np.float64)).astype(BF16)
    return np.concatenate([high, high, low], axis=0)


def azimuth_tables():
    index = np.arange(LANES)
    row = np.arange(AZ_OUTER)[:, None]
    lane = index[None, :]
    grid = index[:, None] * index[None, :]
    forward = split_table(real_form(unit(-grid, LANES)))
    inverse = split_table(real_form(unit(grid, LANES)) / PULSES)
    twiddle_re, twiddle_im = unit(-row * lane, PULSES)
    frequency = row + AZ_OUTER * lane
    doppler = ((frequency + PULSES // 2) % PULSES - PULSES // 2) * (2.0 / PULSES)
    small = np.stack(f32_pair((twiddle_re, twiddle_im)) + (np.asarray(doppler**2, np.float32),))
    eye = np.concatenate([np.eye(LANES), np.eye(LANES)], axis=1).astype(BF16)
    return forward, inverse, small, eye


def times(value, numerator, denominator):
    re, im = value
    eighth = (numerator * 8) / denominator % 8
    if eighth == 0:
        return value
    if eighth == 2:
        return (-im, re)
    if eighth == 4:
        return (-re, -im)
    if eighth == 6:
        return (im, -re)
    half = math.sqrt(0.5)
    if eighth == 1:
        return ((re - im) * half, (re + im) * half)
    if eighth == 3:
        return ((re + im) * -half, (re - im) * half)
    if eighth == 5:
        return ((im - re) * half, (re + im) * -half)
    if eighth == 7:
        return ((re + im) * half, (im - re) * half)
    cosine = math.cos(2.0 * math.pi * numerator / denominator)
    sine = math.sin(2.0 * math.pi * numerator / denominator)
    return (re * cosine - im * sine, re * sine + im * cosine)


def add(one, two):
    return (one[0] + two[0], one[1] + two[1])


def sub(one, two):
    return (one[0] - two[0], one[1] - two[1])


def dft(values, sign):
    count = len(values)
    if count == 1:
        return values
    even = dft(values[0::2], sign)
    odd = dft(values[1::2], sign)
    odd = [times(value, sign * k, count) for k, value in enumerate(odd)]
    return [add(e, o) for e, o in zip(even, odd)] + [sub(e, o) for e, o in zip(even, odd)]


def cmul(one, two):
    return (one[0] * two[0] - one[1] * two[1], one[0] * two[1] + one[1] * two[0])


def first_pass(load, store, count, fine, sign):
    high = count // fine
    for low in range(fine):
        part = dft([load(fine * j + low) for j in range(high)], sign)
        for k, value in enumerate(part):
            store(low, k, times(value, sign * low * k, count))


ROWS = 16


def range_kernel(
    filter_re,
    filter_im,
    weight_re,
    weight_im,
    start_ref,
    table,
    echo_re,
    echo_im,
    out_ref,
    x_re,
    x_im,
    y_ref,
    z_ref,
    tmp_re,
    tmp_im,
    u_ref,
    w_ref,
    sems,
):
    chans, pulses = echo_re.shape[0], echo_re.shape[1]
    per_chan = pulses // ROWS
    chunks = chans * per_chan
    group = lax.axis_index("chan")

    def chunk_copies(i):
        c, r = i // per_chan, i % per_chan
        rows = pl.ds(pl.multiple_of(r * ROWS, ROWS), ROWS)
        return (
            pltpu.make_async_copy(echo_re.at[c, rows], x_re.at[c, rows], sems.at[0, i]),
            pltpu.make_async_copy(echo_im.at[c, rows], x_im.at[c, rows], sems.at[1, i]),
        )

    @pl.loop(0, chunks)
    def _(i):
        for copy in chunk_copies(i):
            copy.start()

    def hdot(one, two):
        return jnp.dot(one, two, precision=lax.Precision.HIGHEST, preferred_element_type=F32)

    ht_re, ht_im = filter_re[...].T, filter_im[...].T
    c_re = jnp.zeros((OUTER, LANES), F32)
    c_im = jnp.zeros((OUTER, LANES), F32)
    for parity in (0, 1):
        rows = slice(parity * OUTER, (parity + 1) * OUTER)
        t_re, t_im = table[2 * parity], table[2 * parity + 1]
        c_re = c_re + hdot(ht_re[rows], t_re) - hdot(ht_im[rows], t_im)
        c_im = c_im + hdot(ht_re[rows], t_im) + hdot(ht_im[rows], t_re)
    upper = cmul((c_re, c_im), (table[4], table[5]))
    lower = cmul((c_re, c_im), (table[6], table[7]))
    u_ref[0], u_ref[1] = upper
    u_ref[2], u_ref[3] = lower

    @pl.loop(0, OUTER)
    def _(a):
        start = start_ref[a]
        for c in range(chans):
            channel = group * chans + c
            live = jnp.logical_and(channel >= start, channel < start + ACTIVE).astype(F32)
            w_ref[0, c, pl.ds(a, 1), :] = weight_re[c, pl.ds(a, 1), :] * live
            w_ref[1, c, pl.ds(a, 1), :] = weight_im[c, pl.ds(a, 1), :] * live

    @pl.loop(0, chunks)
    def _(i):
        for copy in chunk_copies(i):
            copy.wait()
        c, r = i // per_chan, i % per_chan
        rows = pl.ds(pl.multiple_of(r * ROWS, ROWS), ROWS)
        out_rows = pl.ds(pl.multiple_of(i * ROWS, ROWS), ROWS)

        def load(a):
            cols = slice(a * LANES, (a + 1) * LANES)
            return (x_re[c, rows, cols].astype(F32), x_im[c, rows, cols].astype(F32))

        def store(low, k, value):
            tmp_re[0, low * 8 + k] = value[0]
            tmp_im[0, low * 8 + k] = value[1]

        first_pass(load, store, OUTER, 8, -1)
        for k in range(8):
            part = dft([(tmp_re[0, low * 8 + k], tmp_im[0, low * 8 + k]) for low in range(8)], -1)
            for j, value in enumerate(part):
                y_ref[k + 8 * j, out_rows, 0:LANES] = value[0].astype(BF16)
                y_ref[k + 8 * j, out_rows, LANES : 2 * LANES] = value[1].astype(BF16)

    sub_index = lax.broadcasted_iota(jnp.int32, (LANES, LANES), 0)
    lane_index = lax.broadcasted_iota(jnp.int32, (LANES, LANES), 1)
    on_upper = lane_index >= sub_index

    @pl.loop(0, OUTER)
    def _(k):
        def toeplitz(part):
            def rolled(which):
                row = jnp.broadcast_to(u_ref[which, pl.ds(k, 1), :], (LANES, LANES))
                return pltpu.roll(row, 0, 1, stride=1, stride_axis=0)

            return jnp.where(on_upper, rolled(part), rolled(2 + part))

        m_re, m_im = toeplitz(0), toeplitz(1)
        matrix = jnp.concatenate(
            [
                jnp.concatenate([m_re, m_im], axis=1).astype(BF16),
                jnp.concatenate([-m_im, m_re], axis=1).astype(BF16),
            ],
            axis=0,
        )
        z_ref[k] = jnp.dot(y_ref[k], matrix, preferred_element_type=F32)

    low_half = lax.broadcasted_iota(jnp.int32, (ROWS, LANES), 1) < LANES // 2

    @pl.loop(0, per_chan)
    def _(r):
        for c in range(chans):
            in_rows = pl.ds(pl.multiple_of(c * pulses + r * ROWS, ROWS), ROWS)

            def load(k):
                return (z_ref[k, in_rows, 0:LANES], z_ref[k, in_rows, LANES : 2 * LANES])

            def store(low, k, value):
                tmp_re[c, low * 8 + k] = value[0]
                tmp_im[c, low * 8 + k] = value[1]

            first_pass(load, store, OUTER, 8, 1)
        rows = pl.ds(pl.multiple_of(r * ROWS, ROWS), ROWS)
        for k in range(8):
            total = None
            for c in range(chans):
                part = dft([(tmp_re[c, low * 8 + k], tmp_im[c, low * 8 + k]) for low in range(8)], 1)
                weighted = []
                for j, value in enumerate(part):
                    a = k + 8 * j
                    weight = (w_ref[0, c, a : a + 1, :], w_ref[1, c, a : a + 1, :])
                    weighted.append(cmul(value, weight))
                total = weighted if total is None else [add(o, t) for o, t in zip(total, weighted)]
            for j, (re, im) in enumerate(total):
                a = k + 8 * j
                half = LANES // 2
                first = jnp.where(low_half, re, pltpu.roll(im, half, 1))
                second = jnp.where(low_half, pltpu.roll(re, half, 1), im)
                out_ref[2 * a, rows, :] = first.astype(BF16)
                out_ref[2 * a + 1, rows, :] = second.astype(BF16)


def range_call(echo_re, echo_im, filter_re, filter_im, weight_re, weight_im, window_start):
    chans, pulses, samples = echo_re.shape
    vmem = pl.BlockSpec(memory_space=VMEM)
    smem = pl.BlockSpec(memory_space=pltpu.SMEM)
    hbm = pl.BlockSpec(memory_space=pl.ANY)
    chunks = chans * pulses // ROWS
    return pl.pallas_call(
        range_kernel,
        out_shape=jax.ShapeDtypeStruct((2 * OUTER, pulses, LANES), BF16),
        in_specs=[vmem, vmem, vmem, vmem, smem, vmem, hbm, hbm],
        out_specs=vmem,
        scratch_shapes=[
            VMEM((chans, pulses, samples), BF16),
            VMEM((chans, pulses, samples), BF16),
            VMEM((OUTER, chans * pulses, 2 * LANES), BF16),
            VMEM((OUTER, chans * pulses, 2 * LANES), F32),
            VMEM((chans, OUTER, ROWS, LANES), F32),
            VMEM((chans, OUTER, ROWS, LANES), F32),
            VMEM((4, OUTER, LANES), F32),
            VMEM((2, chans, OUTER, LANES), F32),
            pltpu.SemaphoreType.DMA((2, chunks)),
        ],
        compiler_params=pltpu.CompilerParams(vmem_limit_bytes=56 * MIB),
        name="range_compress",
    )(
        filter_re.reshape(OUTER, LANES),
        filter_im.reshape(OUTER, LANES),
        weight_re.reshape(chans, OUTER, LANES),
        weight_im.reshape(chans, OUTER, LANES),
        window_start,
        jnp.asarray(range_tables()),
        echo_re,
        echo_im,
    )


PIECES = 4


def exchange_kernel(part_ref, out_ref, from_sibling, summed, sib_send, sib_recv, send, recv, own):
    chan = lax.axis_index("chan")
    pulse = lax.axis_index("pulse")
    high, core = chan // 2, chan % 2
    sibling = 2 * high + (1 - core)
    count = 2 * AZ_OUTER
    me = high * AZ_OUTER + pulse
    barrier = pltpu.get_barrier_semaphore()

    def partner(t):
        other = (me + t) % count
        return other // AZ_OUTER, other % AZ_OUTER

    pl.semaphore_signal(barrier, inc=1, device_id=(sibling, pulse), device_id_type=MESH)

    @pl.loop(1, count)
    def _(t):
        to_high, to_pulse = partner(t)
        pl.semaphore_signal(
            barrier, inc=1, device_id=(2 * to_high + core, to_pulse), device_id_type=MESH
        )

    pl.semaphore_wait(barrier, count)

    step = AZ_OUTER // PIECES

    def sibling_copy(high_to, piece):
        blocks = pl.ds(piece * step, step)
        return pltpu.make_async_remote_copy(
            src_ref=part_ref.at[high_to, 1 - core, blocks],
            dst_ref=from_sibling.at[high_to, blocks],
            send_sem=sib_send.at[high_to * PIECES + piece],
            recv_sem=sib_recv.at[high_to * PIECES + piece],
            device_id=(sibling, pulse),
            device_id_type=MESH,
        )

    for high_to in range(2):
        for piece in range(PIECES):
            sibling_copy(high_to, piece).start()

    for high_to in range(2):
        for piece in range(PIECES):
            sibling_copy(high_to, piece).wait_recv()

            @pl.loop(piece * step, (piece + 1) * step)
            def _(j):
                total = part_ref[high_to, core, j].astype(F32) + from_sibling[high_to, j].astype(F32)
                summed[high_to, j] = total.astype(BF16)

    def block_copy(t):
        to_high, to_pulse = partner(t)
        return pltpu.make_async_remote_copy(
            src_ref=summed.at[to_high, to_pulse],
            dst_ref=out_ref.at[high, pulse],
            send_sem=send.at[t],
            recv_sem=recv.at[t],
            device_id=(2 * to_high + core, to_pulse),
            device_id_type=MESH,
        )

    @pl.loop(1, count)
    def _(t):
        block_copy(t).start()

    keep = pltpu.make_async_copy(summed.at[high, pulse], out_ref.at[high, pulse], own)
    keep.start()
    keep.wait()

    @pl.loop(1, count)
    def _(t):
        block_copy(t).wait()

    for high_to in range(2):
        for piece in range(PIECES):
            sibling_copy(high_to, piece).wait_send()


def exchange_call(part):
    pulses = part.shape[1]
    vmem = pl.BlockSpec(memory_space=VMEM)
    count = 2 * AZ_OUTER
    return pl.pallas_call(
        exchange_kernel,
        out_shape=jax.ShapeDtypeStruct((2, AZ_OUTER, pulses, LANES), BF16),
        in_specs=[vmem],
        out_specs=vmem,
        scratch_shapes=[
            VMEM((2, AZ_OUTER, pulses, LANES), BF16),
            VMEM((2, AZ_OUTER, pulses, LANES), BF16),
            pltpu.SemaphoreType.DMA((2 * PIECES,)),
            pltpu.SemaphoreType.DMA((2 * PIECES,)),
            pltpu.SemaphoreType.DMA((count,)),
            pltpu.SemaphoreType.DMA((count,)),
            pltpu.SemaphoreType.DMA,
        ],
        compiler_params=pltpu.CompilerParams(
            collective_id=0, has_side_effects=True, vmem_limit_bytes=32 * MIB
        ),
        name="exchange",
    )(part.reshape(2, 2, AZ_OUTER, pulses, LANES))


def unit_of_half_turns(turns):
    quarter = jnp.floor(turns * 2.0 + 0.5)
    x = (turns - quarter * 0.5) * math.pi
    y = x * x
    sine = x * (1.0 + y * (-1.0 / 6 + y * (1.0 / 120 + y * (-1.0 / 5040 + y * (1.0 / 362880)))))
    cosine = 1.0 + y * (-0.5 + y * (1.0 / 24 + y * (-1.0 / 720 + y * (1.0 / 40320))))
    index = quarter.astype(jnp.int32)
    swap = index % 2 == 1
    one = jnp.where(swap, sine, cosine)
    two = jnp.where(swap, cosine, sine)
    one = jnp.where((index + 1) // 2 % 2 == 1, -one, one)
    two = jnp.where(index // 2 % 2 == 1, -two, two)
    return one, two


GROUP = 4


def split_dot(x, table):
    high = x.astype(BF16)
    low = (x - high.astype(F32)).astype(BF16)
    return jnp.dot(
        jnp.concatenate([high, low, high], axis=1), table, preferred_element_type=F32
    )


def azimuth_kernel(
    beam, filter_re, filter_im, rate, forward, inverse, small, eye, out_re, out_im, a_ref, b_ref, tmp_re, tmp_im
):
    cols = out_re.shape[0]
    twiddle_re, twiddle_im, doppler2 = small.at[0], small.at[1], small.at[2]

    @pl.loop(0, AZ_OUTER)
    def _(s):
        both = jnp.concatenate([beam[0, s], beam[1, s]], axis=1)
        a_ref[s] = lax.dot_general(
            eye[...], both, (((1,), (1,)), ((), ())), preferred_element_type=F32
        )

    def stash(low, k, value):
        tmp_re[low * 8 + k] = value[0]
        tmp_im[low * 8 + k] = value[1]

    def second(k, sign):
        return dft([(tmp_re[low * 8 + k], tmp_im[low * 8 + k]) for low in range(4)], sign)

    @pl.loop(0, cols // 8)
    def _(r):
        re_rows = pl.ds(pl.multiple_of(r * 8, 8), 8)
        im_rows = pl.ds(pl.multiple_of(cols + r * 8, 8), 8)
        first_pass(lambda s: (a_ref[s, re_rows, :], a_ref[s, im_rows, :]), stash, AZ_OUTER, 4, -1)
        for k in range(8):
            for j, value in enumerate(second(k, -1)):
                at = k + 8 * j
                re, im = cmul(value, (twiddle_re[at : at + 1, :], twiddle_im[at : at + 1, :]))
                b_ref[at, re_rows, 0:LANES] = re
                b_ref[at, re_rows, LANES : 2 * LANES] = im

    rate_lanes = jnp.broadcast_to(rate[...], (cols, LANES))

    @pl.loop(0, AZ_OUTER // GROUP)
    def _(g):
        at = pl.ds(g * GROUP, GROUP)
        x = b_ref[at].reshape(GROUP * cols, 2 * LANES)
        s = split_dot(x, forward[...]).reshape(GROUP, cols, 2 * LANES)
        parts = []
        for i in range(GROUP):
            turns = rate_lanes * doppler2[pl.ds(g * GROUP + i, 1), :]
            cosine, sine = unit_of_half_turns(turns)
            gain_re, gain_im = filter_re[g * GROUP + i], filter_im[g * GROUP + i]
            factor = (cosine * gain_re + sine * gain_im, cosine * gain_im - sine * gain_re)
            re, im = cmul((s[i, :, 0:LANES], s[i, :, LANES : 2 * LANES]), factor)
            parts.append(jnp.concatenate([re, im], axis=1))
        focused = split_dot(jnp.concatenate(parts, axis=0), inverse[...])
        b_ref[at] = focused.reshape(GROUP, cols, 2 * LANES)

    @pl.loop(0, cols // 8)
    def _(r):
        rows = pl.ds(pl.multiple_of(r * 8, 8), 8)

        def load(k):
            value = (b_ref[k, rows, 0:LANES], b_ref[k, rows, LANES : 2 * LANES])
            return cmul(value, (twiddle_re[k : k + 1, :], -twiddle_im[k : k + 1, :]))

        first_pass(load, stash, AZ_OUTER, 4, 1)
        for k in range(8):
            for j, value in enumerate(second(k, 1)):
                s = k + 8 * j
                out_re[rows, s * LANES : (s + 1) * LANES] = value[0]
                out_im[rows, s * LANES : (s + 1) * LANES] = value[1]


def azimuth_call(beam, filter_re, filter_im, rate):
    cols = rate.shape[0]
    forward, inverse, small, eye = azimuth_tables()
    shape = jax.ShapeDtypeStruct((cols, PULSES), F32)
    vmem = pl.BlockSpec(memory_space=VMEM)

    def by_outer(part):
        return part.reshape(cols, LANES, AZ_OUTER).transpose(2, 0, 1)

    return pl.pallas_call(
        azimuth_kernel,
        out_shape=(shape, shape),
        in_specs=[vmem] * 8,
        out_specs=(vmem, vmem),
        scratch_shapes=[
            VMEM((AZ_OUTER, 2 * cols, LANES), F32),
            VMEM((AZ_OUTER, cols, 2 * LANES), F32),
            VMEM((AZ_OUTER, 8, LANES), F32),
            VMEM((AZ_OUTER, 8, LANES), F32),
        ],
        compiler_params=pltpu.CompilerParams(vmem_limit_bytes=32 * MIB),
        name="azimuth_focus",
    )(
        beam,
        by_outer(filter_re),
        by_outer(filter_im),
        rate.reshape(cols, 1),
        jnp.asarray(forward),
        jnp.asarray(inverse),
        jnp.asarray(small),
        jnp.asarray(eye),
    )


def local(
    echo_re,
    echo_im,
    range_filter_re,
    range_filter_im,
    beam_weight_re,
    beam_weight_im,
    window_start,
    azimuth_filter_re,
    azimuth_filter_im,
    migration_rate,
):
    part = range_call(
        echo_re,
        echo_im,
        range_filter_re,
        range_filter_im,
        beam_weight_re,
        beam_weight_im,
        window_start,
    )
    beam = exchange_call(part)
    return azimuth_call(beam, azimuth_filter_re, azimuth_filter_im, migration_rate)


def solution(mesh):
    placed = (
        P("chan", "pulse", None),
        P("chan", "pulse", None),
        P(),
        P(),
        P("chan", None),
        P("chan", None),
        P(),
        P(("chan", "pulse"), None),
        P(("chan", "pulse"), None),
        P(("chan", "pulse")),
    )
    return jax.shard_map(
        local,
        mesh=mesh,
        in_specs=placed,
        out_specs=(P(("chan", "pulse"), None), P(("chan", "pulse"), None)),
        check_vma=False,
    )
```

```python
import functools
import math

import jax
import jax.numpy as jnp
import numpy as np
from jax import lax
from jax.experimental import pallas as pl
from jax.experimental.pallas import tpu as pltpu
from jax.sharding import PartitionSpec as P

ACTIVE = 4
F32 = jnp.float32
BF16 = jnp.bfloat16
MESH = pl.DeviceIdType.MESH
VMEM = pltpu.VMEM
MIB = 1024 * 1024

OUTER = 64
LANES = 128
RANGE = OUTER * LANES
AZ_OUTER = 32
PULSES = AZ_OUTER * LANES


def unit(numerator, denominator):
    angle = 2.0 * np.pi * (np.asarray(numerator) % denominator) / denominator
    return np.cos(angle), np.sin(angle)


def f32_pair(pair):
    return tuple(np.asarray(part, np.float32) for part in pair)


def range_tables():
    row = np.arange(OUTER)[:, None]
    lane = np.arange(LANES)[None, :]
    tables = []
    for parity in (0, 1):
        re, im = unit(lane * (2 * row + parity), LANES)
        tables += f32_pair((re / RANGE, im / RANGE))
    tables += f32_pair(unit(row * lane, RANGE))
    tables += f32_pair(unit(row * (lane - LANES), RANGE))
    return np.stack(tables)


def real_form(pair):
    re, im = pair
    return np.block([[re, im], [-im, re]])


def split_table(table):
    high = table.astype(BF16)
    low = (table - high.astype(np.float64)).astype(BF16)
    return np.concatenate([high, high, low], axis=0)


def azimuth_tables():
    index = np.arange(LANES)
    row = np.arange(AZ_OUTER)[:, None]
    lane = index[None, :]
    grid = index[:, None] * index[None, :]
    forward = split_table(real_form(unit(-grid, LANES)))
    inverse = split_table(real_form(unit(grid, LANES)) / PULSES)
    twiddle_re, twiddle_im = unit(-row * lane, PULSES)
    frequency = row + AZ_OUTER * lane
    doppler = ((frequency + PULSES // 2) % PULSES - PULSES // 2) * (2.0 / PULSES)
    small = np.stack(f32_pair((twiddle_re, twiddle_im)) + (np.asarray(doppler**2, np.float32),))
    eye = np.concatenate([np.eye(LANES), np.eye(LANES)], axis=1).astype(BF16)
    return forward, inverse, small, eye


def times(value, numerator, denominator):
    re, im = value
    eighth = (numerator * 8) / denominator % 8
    if eighth == 0:
        return value
    if eighth == 2:
        return (-im, re)
    if eighth == 4:
        return (-re, -im)
    if eighth == 6:
        return (im, -re)
    half = math.sqrt(0.5)
    if eighth == 1:
        return ((re - im) * half, (re + im) * half)
    if eighth == 3:
        return ((re + im) * -half, (re - im) * half)
    if eighth == 5:
        return ((im - re) * half, (re + im) * -half)
    if eighth == 7:
        return ((re + im) * half, (im - re) * half)
    cosine = math.cos(2.0 * math.pi * numerator / denominator)
    sine = math.sin(2.0 * math.pi * numerator / denominator)
    return (re * cosine - im * sine, re * sine + im * cosine)


def add(one, two):
    return (one[0] + two[0], one[1] + two[1])


def sub(one, two):
    return (one[0] - two[0], one[1] - two[1])


def dft(values, sign):
    count = len(values)
    if count == 1:
        return values
    even = dft(values[0::2], sign)
    odd = dft(values[1::2], sign)
    odd = [times(value, sign * k, count) for k, value in enumerate(odd)]
    return [add(e, o) for e, o in zip(even, odd)] + [sub(e, o) for e, o in zip(even, odd)]


def cmul(one, two):
    return (one[0] * two[0] - one[1] * two[1], one[0] * two[1] + one[1] * two[0])


def first_pass(load, store, count, fine, sign):
    high = count // fine
    for low in range(fine):
        part = dft([load(fine * j + low) for j in range(high)], sign)
        for k, value in enumerate(part):
            store(low, k, times(value, sign * low * k, count))


def unit_of_half_turns(turns):
    quarter = jnp.floor(turns * 2.0 + 0.5)
    x = (turns - quarter * 0.5) * math.pi
    y = x * x
    sine = x * (1.0 + y * (-1.0 / 6 + y * (1.0 / 120 + y * (-1.0 / 5040 + y * (1.0 / 362880)))))
    cosine = 1.0 + y * (-0.5 + y * (1.0 / 24 + y * (-1.0 / 720 + y * (1.0 / 40320))))
    index = quarter.astype(jnp.int32)
    swap = index % 2 == 1
    one = jnp.where(swap, sine, cosine)
    two = jnp.where(swap, cosine, sine)
    one = jnp.where((index + 1) // 2 % 2 == 1, -one, one)
    two = jnp.where(index // 2 % 2 == 1, -two, two)
    return one, two


ROWS = 16
CHUNKS = 4
OFFSETS = sorted(
    [(x, y, z) for x in range(4) for y in range(4) for z in range(4) if (x, y, z) != (0, 0, 0)],
    key=lambda offset: -sum(min(d, 4 - d) for d in offset),
)


def place():
    chan, pulse = lax.axis_index("chan"), lax.axis_index("pulse")
    return (chan // 2) * 2 + pulse // 16, (pulse // 4) % 4, pulse % 4, chan % 2


def device_at(x, y, z, core):
    return ((x // 2) * 2 + core, (x % 2) * 16 + y * 4 + z)


def range_kernel(
    filter_re,
    filter_im,
    weight_re,
    weight_im,
    start_ref,
    table,
    rate,
    doppler2,
    echo_re,
    echo_im,
    gain_re,
    gain_im,
    beam_ref,
    factor_re,
    factor_im,
    x_re,
    x_im,
    y_ref,
    z_ref,
    m_ref,
    tmp_re,
    tmp_im,
    u_ref,
    w_ref,
    g_re,
    g_im,
    q_ref,
    part_ref,
    from_sibling,
    summed,
    echo_sems,
    gain_sems,
    sib_send,
    sib_recv,
    send,
    recv,
    own,
):
    chans, pulses = echo_re.shape[0], echo_re.shape[1]
    chunk_rows = pulses // CHUNKS
    per_chan = chunk_rows // ROWS
    cols = rate.shape[0]
    chan, pulse = lax.axis_index("chan"), lax.axis_index("pulse")
    x, y, z, core = place()
    high = x // 2
    sibling = device_at(x, y, z, 1 - core)

    def target(offset):
        return (x + offset[0]) % 4, (y + offset[1]) % 4, (z + offset[2]) % 4

    barrier = pltpu.get_barrier_semaphore()
    pl.semaphore_signal(barrier, inc=1, device_id=sibling, device_id_type=MESH)
    for offset in OFFSETS:
        pl.semaphore_signal(
            barrier, inc=1, device_id=device_at(*target(offset), core), device_id_type=MESH
        )

    def echo_copies(i):
        rows = pl.ds(pl.multiple_of(i * chunk_rows, chunk_rows), chunk_rows)
        return (
            pltpu.make_async_copy(echo_re.at[:, rows], x_re.at[:, rows], echo_sems.at[0, i]),
            pltpu.make_async_copy(echo_im.at[:, rows], x_im.at[:, rows], echo_sems.at[1, i]),
        )

    @pl.loop(0, CHUNKS)
    def _(i):
        for copy in echo_copies(i):
            copy.start()

    gain_copies = (
        pltpu.make_async_copy(gain_re, g_re, gain_sems.at[0]),
        pltpu.make_async_copy(gain_im, g_im, gain_sems.at[1]),
    )
    for copy in gain_copies:
        copy.start()

    def hdot(one, two):
        return jnp.dot(one, two, precision=lax.Precision.HIGHEST, preferred_element_type=F32)

    ht_re, ht_im = filter_re[...].T, filter_im[...].T
    c_re = jnp.zeros((OUTER, LANES), F32)
    c_im = jnp.zeros((OUTER, LANES), F32)
    for parity in (0, 1):
        rows = slice(parity * OUTER, (parity + 1) * OUTER)
        t_re, t_im = table[2 * parity], table[2 * parity + 1]
        c_re = c_re + hdot(ht_re[rows], t_re) - hdot(ht_im[rows], t_im)
        c_im = c_im + hdot(ht_re[rows], t_im) + hdot(ht_im[rows], t_re)
    upper = cmul((c_re, c_im), (table[4], table[5]))
    lower = cmul((c_re, c_im), (table[6], table[7]))
    u_ref[0], u_ref[1] = upper
    u_ref[2], u_ref[3] = lower

    @pl.loop(0, OUTER, unroll=4)
    def _(a):
        start = start_ref[a]
        for c in range(chans):
            channel = chan * chans + c
            live = jnp.logical_and(channel >= start, channel < start + ACTIVE).astype(F32)
            w_ref[0, c, pl.ds(a, 1), :] = weight_re[c, pl.ds(a, 1), :] * live
            w_ref[1, c, pl.ds(a, 1), :] = weight_im[c, pl.ds(a, 1), :] * live

    sub_index = lax.broadcasted_iota(jnp.int32, (LANES, LANES), 0)
    lane_index = lax.broadcasted_iota(jnp.int32, (LANES, LANES), 1)
    on_upper = lane_index >= sub_index

    @pl.loop(0, OUTER, unroll=4)
    def _(k):
        def toeplitz(part):
            def rolled(which):
                row = jnp.broadcast_to(u_ref[which, pl.ds(k, 1), :], (LANES, LANES))
                return pltpu.roll(row, 0, 1, stride=1, stride_axis=0)

            return jnp.where(on_upper, rolled(part), rolled(2 + part))

        m_re, m_im = toeplitz(0), toeplitz(1)
        m_ref[k, 0:LANES, 0:LANES] = m_re.astype(BF16)
        m_ref[k, 0:LANES, LANES : 2 * LANES] = m_im.astype(BF16)
        m_ref[k, LANES : 2 * LANES, 0:LANES] = (-m_im).astype(BF16)
        m_ref[k, LANES : 2 * LANES, LANES : 2 * LANES] = m_re.astype(BF16)

    def outer_forward(i):
        for copy in echo_copies(i):
            copy.wait()

        @pl.loop(0, chans * per_chan)
        def _(it):
            c, r = it // per_chan, it % per_chan
            rows = pl.ds(pl.multiple_of(i * chunk_rows + r * ROWS, ROWS), ROWS)
            out_rows = pl.ds(pl.multiple_of(it * ROWS, ROWS), ROWS)

            def load(a):
                lanes = slice(a * LANES, (a + 1) * LANES)
                return (x_re[c, rows, lanes].astype(F32), x_im[c, rows, lanes].astype(F32))

            def store(low, k, value):
                tmp_re[0, low * 8 + k] = value[0]
                tmp_im[0, low * 8 + k] = value[1]

            first_pass(load, store, OUTER, 8, -1)
            for k in range(8):
                part = dft([(tmp_re[0, low * 8 + k], tmp_im[0, low * 8 + k]) for low in range(8)], -1)
                for j, value in enumerate(part):
                    y_ref[k + 8 * j, out_rows, 0:LANES] = value[0].astype(BF16)
                    y_ref[k + 8 * j, out_rows, LANES : 2 * LANES] = value[1].astype(BF16)

    def filter_inner():
        @pl.loop(0, OUTER, unroll=8)
        def _(k):
            z_ref[k] = jnp.dot(y_ref[k], m_ref[k], preferred_element_type=F32)

    low_half = lax.broadcasted_iota(jnp.int32, (ROWS, LANES), 1) < LANES // 2

    def outer_inverse(i):
        @pl.loop(0, per_chan)
        def _(r):
            for c in range(chans):
                in_rows = pl.ds(pl.multiple_of(c * chunk_rows + r * ROWS, ROWS), ROWS)

                def load(k):
                    return (z_ref[k, in_rows, 0:LANES], z_ref[k, in_rows, LANES : 2 * LANES])

                def store(low, k, value):
                    tmp_re[c, low * 8 + k] = value[0]
                    tmp_im[c, low * 8 + k] = value[1]

                first_pass(load, store, OUTER, 8, 1)
            rows = pl.ds(pl.multiple_of(r * ROWS, ROWS), ROWS)
            for k in range(8):
                total = None
                for c in range(chans):
                    part = dft(
                        [(tmp_re[c, low * 8 + k], tmp_im[c, low * 8 + k]) for low in range(8)], 1
                    )
                    weighted = []
                    for j, value in enumerate(part):
                        a = k + 8 * j
                        weight = (w_ref[0, c, a : a + 1, :], w_ref[1, c, a : a + 1, :])
                        weighted.append(cmul(value, weight))
                    total = weighted if total is None else [add(o, t) for o, t in zip(total, weighted)]
                for j, (re, im) in enumerate(total):
                    half = LANES // 2
                    first = jnp.where(low_half, re, pltpu.roll(im, half, 1))
                    second = jnp.where(low_half, pltpu.roll(re, half, 1), im)
                    for side, value in enumerate((first, second)):
                        owner = 2 * (k + 8 * j) + side
                        to_high, to_core, to_pulse = owner // 64, owner // 32 % 2, owner % 32
                        part_ref[i, to_high, to_core, to_pulse, rows, :] = value.astype(BF16)

    def sibling_copy(i, to_high):
        return pltpu.make_async_remote_copy(
            src_ref=part_ref.at[i, to_high, 1 - core],
            dst_ref=from_sibling.at[i, to_high],
            send_sem=sib_send.at[i, to_high],
            recv_sem=sib_recv.at[i, to_high],
            device_id=sibling,
            device_id_type=MESH,
        )

    def block_copy(i, n):
        to_x, to_y, to_z = target(OFFSETS[n])
        return pltpu.make_async_remote_copy(
            src_ref=summed.at[i, to_x // 2, (to_x % 2) * 16 + to_y * 4 + to_z],
            dst_ref=beam_ref.at[i, high, pulse],
            send_sem=send.at[i, n],
            recv_sem=recv.at[i, n],
            device_id=device_at(to_x, to_y, to_z, core),
            device_id_type=MESH,
        )

    def own_copy(i):
        return pltpu.make_async_copy(
            summed.at[i, high, pulse], beam_ref.at[i, high, pulse], own.at[i]
        )

    def send_blocks(i):
        for to_high in range(2):
            sibling_copy(i, to_high).wait_recv()

            @pl.loop(0, AZ_OUTER, unroll=8)
            def _(j):
                mine = part_ref[i, to_high, core, j].astype(F32)
                summed[i, to_high, j] = (mine + from_sibling[i, to_high, j].astype(F32)).astype(BF16)

        for n in range(len(OFFSETS)):
            block_copy(i, n).start()
        own_copy(i).start()

    def azimuth_factor():
        for copy in gain_copies:
            copy.wait()

        @pl.loop(0, AZ_OUTER, unroll=4)
        def _(j):
            lanes = pl.ds(pl.multiple_of(j * LANES, LANES), LANES)
            q_ref[lanes, :] = jnp.concatenate([g_re[:, lanes], g_im[:, lanes]], axis=0).T

        rate_lanes = jnp.broadcast_to(rate[...], (cols, LANES))

        @pl.loop(0, AZ_OUTER, unroll=2)
        def _(k):
            gains = q_ref[pl.ds(k, LANES, stride=AZ_OUTER), :].T
            cosine, sine = unit_of_half_turns(rate_lanes * doppler2[pl.ds(k, 1), :])
            re, im = gains[0:cols], gains[cols : 2 * cols]
            factor_re[k] = cosine * re + sine * im
            factor_im[k] = cosine * im - sine * re

    pl.semaphore_wait(barrier, len(OFFSETS) + 1)

    @pl.loop(0, CHUNKS + 1)
    def _(i):
        @pl.when(i < CHUNKS)
        def _():
            outer_forward(i)

        @pl.when(i == CHUNKS)
        def _():
            azimuth_factor()

        @pl.when(i > 0)
        def _():
            send_blocks(i - 1)

        @pl.when(i < CHUNKS)
        def _():
            filter_inner()
            outer_inverse(i)
            for to_high in range(2):
                sibling_copy(i, to_high).start()

    @pl.loop(0, CHUNKS)
    def _(i):
        for n in range(len(OFFSETS)):
            block_copy(i, n).wait()
        own_copy(i).wait()
        for to_high in range(2):
            sibling_copy(i, to_high).wait_send()


def range_call(
    echo_re, echo_im, filter_re, filter_im, weight_re, weight_im, window_start, gain_re, gain_im, rate
):
    chans, pulses, samples = echo_re.shape
    cols = rate.shape[0]
    chunk_rows = pulses // CHUNKS
    vmem = pl.BlockSpec(memory_space=VMEM)
    smem = pl.BlockSpec(memory_space=pltpu.SMEM)
    hbm = pl.BlockSpec(memory_space=pl.ANY)
    dma = pltpu.SemaphoreType.DMA
    factor = jax.ShapeDtypeStruct((AZ_OUTER, cols, LANES), F32)
    return pl.pallas_call(
        range_kernel,
        out_shape=(
            jax.ShapeDtypeStruct((CHUNKS, 2, AZ_OUTER, chunk_rows, LANES), BF16),
            factor,
            factor,
        ),
        in_specs=[vmem, vmem, vmem, vmem, smem, vmem, vmem, vmem, hbm, hbm, hbm, hbm],
        out_specs=(vmem, vmem, vmem),
        scratch_shapes=[
            VMEM((chans, pulses, samples), BF16),
            VMEM((chans, pulses, samples), BF16),
            VMEM((OUTER, chans * chunk_rows, 2 * LANES), BF16),
            VMEM((OUTER, chans * chunk_rows, 2 * LANES), F32),
            VMEM((OUTER, 2 * LANES, 2 * LANES), BF16),
            VMEM((chans, OUTER, ROWS, LANES), F32),
            VMEM((chans, OUTER, ROWS, LANES), F32),
            VMEM((4, OUTER, LANES), F32),
            VMEM((2, chans, OUTER, LANES), F32),
            VMEM((cols, PULSES), F32),
            VMEM((cols, PULSES), F32),
            VMEM((PULSES, LANES), F32),
            VMEM((CHUNKS, 2, 2, AZ_OUTER, chunk_rows, LANES), BF16),
            VMEM((CHUNKS, 2, AZ_OUTER, chunk_rows, LANES), BF16),
            VMEM((CHUNKS, 2, AZ_OUTER, chunk_rows, LANES), BF16),
            dma((2, CHUNKS)),
            dma((2,)),
            dma((CHUNKS, 2)),
            dma((CHUNKS, 2)),
            dma((CHUNKS, len(OFFSETS))),
            dma((CHUNKS, len(OFFSETS))),
            dma((CHUNKS,)),
        ],
        compiler_params=pltpu.CompilerParams(
            collective_id=0, has_side_effects=True, vmem_limit_bytes=58 * MIB
        ),
        name="range_exchange",
    )(
        filter_re.reshape(OUTER, LANES),
        filter_im.reshape(OUTER, LANES),
        weight_re.reshape(chans, OUTER, LANES),
        weight_im.reshape(chans, OUTER, LANES),
        window_start,
        jnp.asarray(range_tables()),
        rate.reshape(cols, 1),
        jnp.asarray(azimuth_tables()[2][2]),
        echo_re,
        echo_im,
        gain_re,
        gain_im,
    )


GROUP = 4


def split_dot(x, table):
    high = x.astype(BF16)
    low = (x - high.astype(F32)).astype(BF16)
    return jnp.dot(
        jnp.concatenate([high, low, high], axis=1), table, preferred_element_type=F32
    )


def azimuth_kernel(
    beam, factor_re, factor_im, forward, inverse, small, eye, out_re, out_im, a_ref, b_ref, tmp_re, tmp_im
):
    cols = out_re.shape[0]
    twiddle_re, twiddle_im = small.at[0], small.at[1]

    @pl.loop(0, AZ_OUTER, unroll=8)
    def _(s):
        halves = [
            jnp.concatenate([beam[i, high, s] for i in range(beam.shape[0])], axis=0)
            for high in range(2)
        ]
        both = jnp.concatenate(halves, axis=1)
        a_ref[s] = lax.dot_general(
            eye[...], both, (((1,), (1,)), ((), ())), preferred_element_type=F32
        )

    def stash(low, k, value):
        tmp_re[low * 8 + k] = value[0]
        tmp_im[low * 8 + k] = value[1]

    def second(k, sign):
        return dft([(tmp_re[low * 8 + k], tmp_im[low * 8 + k]) for low in range(4)], sign)

    @pl.loop(0, cols // 8)
    def _(r):
        re_rows = pl.ds(pl.multiple_of(r * 8, 8), 8)
        im_rows = pl.ds(pl.multiple_of(cols + r * 8, 8), 8)
        first_pass(lambda s: (a_ref[s, re_rows, :], a_ref[s, im_rows, :]), stash, AZ_OUTER, 4, -1)
        for k in range(8):
            for j, value in enumerate(second(k, -1)):
                at = k + 8 * j
                re, im = cmul(value, (twiddle_re[at : at + 1, :], twiddle_im[at : at + 1, :]))
                b_ref[at, re_rows, 0:LANES] = re
                b_ref[at, re_rows, LANES : 2 * LANES] = im

    @pl.loop(0, AZ_OUTER // GROUP, unroll=2)
    def _(g):
        at = pl.ds(g * GROUP, GROUP)
        x = b_ref[at].reshape(GROUP * cols, 2 * LANES)
        s = split_dot(x, forward[...]).reshape(GROUP, cols, 2 * LANES)
        parts = []
        for i in range(GROUP):
            factor = (factor_re[g * GROUP + i], factor_im[g * GROUP + i])
            re, im = cmul((s[i, :, 0:LANES], s[i, :, LANES : 2 * LANES]), factor)
            parts.append(jnp.concatenate([re, im], axis=1))
        focused = split_dot(jnp.concatenate(parts, axis=0), inverse[...])
        b_ref[at] = focused.reshape(GROUP, cols, 2 * LANES)

    @pl.loop(0, cols // 8)
    def _(r):
        rows = pl.ds(pl.multiple_of(r * 8, 8), 8)

        def load(k):
            value = (b_ref[k, rows, 0:LANES], b_ref[k, rows, LANES : 2 * LANES])
            return cmul(value, (twiddle_re[k : k + 1, :], -twiddle_im[k : k + 1, :]))

        first_pass(load, stash, AZ_OUTER, 4, 1)
        for k in range(8):
            for j, value in enumerate(second(k, 1)):
                s = k + 8 * j
                out_re[rows, s * LANES : (s + 1) * LANES] = value[0]
                out_im[rows, s * LANES : (s + 1) * LANES] = value[1]


def azimuth_call(beam, factor_re, factor_im):
    cols = factor_re.shape[1]
    forward, inverse, small, eye = azimuth_tables()
    shape = jax.ShapeDtypeStruct((cols, PULSES), F32)
    vmem = pl.BlockSpec(memory_space=VMEM)

    return pl.pallas_call(
        azimuth_kernel,
        out_shape=(shape, shape),
        in_specs=[vmem] * 7,
        out_specs=(vmem, vmem),
        scratch_shapes=[
            VMEM((AZ_OUTER, 2 * cols, LANES), F32),
            VMEM((AZ_OUTER, cols, 2 * LANES), F32),
            VMEM((AZ_OUTER, 8, LANES), F32),
            VMEM((AZ_OUTER, 8, LANES), F32),
        ],
        compiler_params=pltpu.CompilerParams(vmem_limit_bytes=32 * MIB),
        name="azimuth_focus",
    )(
        beam,
        factor_re,
        factor_im,
        jnp.asarray(forward),
        jnp.asarray(inverse),
        jnp.asarray(small),
        jnp.asarray(eye),
    )


def local(
    echo_re,
    echo_im,
    range_filter_re,
    range_filter_im,
    beam_weight_re,
    beam_weight_im,
    window_start,
    azimuth_filter_re,
    azimuth_filter_im,
    migration_rate,
):
    beam, factor_re, factor_im = range_call(
        echo_re,
        echo_im,
        range_filter_re,
        range_filter_im,
        beam_weight_re,
        beam_weight_im,
        window_start,
        azimuth_filter_re,
        azimuth_filter_im,
        migration_rate,
    )
    return azimuth_call(beam, factor_re, factor_im)


def solution(mesh):
    placed = (
        P("chan", "pulse", None),
        P("chan", "pulse", None),
        P(),
        P(),
        P("chan", None),
        P("chan", None),
        P(),
        P(("chan", "pulse"), None),
        P(("chan", "pulse"), None),
        P(("chan", "pulse")),
    )
    return jax.shard_map(
        local,
        mesh=mesh,
        in_specs=placed,
        out_specs=(P(("chan", "pulse"), None), P(("chan", "pulse"), None)),
        check_vma=False,
    )
```

```python
import functools
import math

import jax
import jax.numpy as jnp
import numpy as np
from jax import lax
from jax.experimental import pallas as pl
from jax.experimental.pallas import tpu as pltpu
from jax.sharding import PartitionSpec as P

ACTIVE = 4
F32 = jnp.float32
BF16 = jnp.bfloat16
MESH = pl.DeviceIdType.MESH
VMEM = pltpu.VMEM
MIB = 1024 * 1024

OUTER = 64
LANES = 128
RANGE = OUTER * LANES
AZ_OUTER = 32
PULSES = AZ_OUTER * LANES


def unit(numerator, denominator):
    angle = 2.0 * np.pi * (np.asarray(numerator) % denominator) / denominator
    return np.cos(angle), np.sin(angle)


def f32_pair(pair):
    return tuple(np.asarray(part, np.float32) for part in pair)


def range_tables():
    row = np.arange(OUTER)[:, None]
    lane = np.arange(LANES)[None, :]
    tables = []
    for parity in (0, 1):
        re, im = unit(lane * (2 * row + parity), LANES)
        tables += f32_pair((re / RANGE, im / RANGE))
    tables += f32_pair(unit(row * lane, RANGE))
    tables += f32_pair(unit(row * (lane - LANES), RANGE))
    return np.stack(tables)


def real_form(pair):
    re, im = pair
    return np.block([[re, im], [-im, re]])


def split_table(table):
    high = table.astype(BF16)
    low = (table - high.astype(np.float64)).astype(BF16)
    return np.concatenate([high, high, low], axis=0)


def azimuth_tables():
    index = np.arange(LANES)
    row = np.arange(AZ_OUTER)[:, None]
    lane = index[None, :]
    grid = index[:, None] * index[None, :]
    forward = split_table(real_form(unit(-grid, LANES)))
    inverse = split_table(real_form(unit(grid, LANES)) / PULSES)
    twiddle_re, twiddle_im = unit(-row * lane, PULSES)
    frequency = row + AZ_OUTER * lane
    doppler = ((frequency + PULSES // 2) % PULSES - PULSES // 2) * (2.0 / PULSES)
    small = np.stack(f32_pair((twiddle_re, twiddle_im)) + (np.asarray(doppler**2, np.float32),))
    eye = np.eye(LANES).astype(BF16)
    return forward, inverse, small, eye


def times(value, numerator, denominator):
    re, im = value
    eighth = (numerator * 8) / denominator % 8
    if eighth == 0:
        return value
    if eighth == 2:
        return (-im, re)
    if eighth == 4:
        return (-re, -im)
    if eighth == 6:
        return (im, -re)
    half = math.sqrt(0.5)
    if eighth == 1:
        return ((re - im) * half, (re + im) * half)
    if eighth == 3:
        return ((re + im) * -half, (re - im) * half)
    if eighth == 5:
        return ((im - re) * half, (re + im) * -half)
    if eighth == 7:
        return ((re + im) * half, (im - re) * half)
    cosine = math.cos(2.0 * math.pi * numerator / denominator)
    sine = math.sin(2.0 * math.pi * numerator / denominator)
    return (re * cosine - im * sine, re * sine + im * cosine)


def add(one, two):
    return (one[0] + two[0], one[1] + two[1])


def sub(one, two):
    return (one[0] - two[0], one[1] - two[1])


def dft(values, sign):
    count = len(values)
    if count == 1:
        return values
    even = dft(values[0::2], sign)
    odd = dft(values[1::2], sign)
    odd = [times(value, sign * k, count) for k, value in enumerate(odd)]
    return [add(e, o) for e, o in zip(even, odd)] + [sub(e, o) for e, o in zip(even, odd)]


def cmul(one, two):
    return (one[0] * two[0] - one[1] * two[1], one[0] * two[1] + one[1] * two[0])


def first_pass(load, store, count, fine, sign):
    high = count // fine
    for low in range(fine):
        part = dft([load(fine * j + low) for j in range(high)], sign)
        for k, value in enumerate(part):
            store(low, k, times(value, sign * low * k, count))


def unit_of_half_turns(turns):
    quarter = jnp.floor(turns * 2.0 + 0.5)
    x = (turns - quarter * 0.5) * math.pi
    y = x * x
    sine = x * (1.0 + y * (-1.0 / 6 + y * (1.0 / 120 + y * (-1.0 / 5040 + y * (1.0 / 362880)))))
    cosine = 1.0 + y * (-0.5 + y * (1.0 / 24 + y * (-1.0 / 720 + y * (1.0 / 40320))))
    index = quarter.astype(jnp.int32)
    swap = index % 2 == 1
    one = jnp.where(swap, sine, cosine)
    two = jnp.where(swap, cosine, sine)
    one = jnp.where((index + 1) // 2 % 2 == 1, -one, one)
    two = jnp.where(index // 2 % 2 == 1, -two, two)
    return one, two


ROWS = 16
CHUNKS = 4
X_OFFSETS = (2, 1, 3)
YZ_OFFSETS = sorted(
    [(y, z) for y in range(4) for z in range(4) if (y, z) != (0, 0)],
    key=lambda offset: -sum(min(d, 4 - d) for d in offset),
)
YZ = 16


def place():
    chan, pulse = lax.axis_index("chan"), lax.axis_index("pulse")
    return (chan // 2) * 2 + pulse // 16, (pulse // 4) % 4, pulse % 4, chan % 2


def device_at(x, y, z, core):
    return ((x // 2) * 2 + core, (x % 2) * 16 + y * 4 + z)


def range_kernel(
    filter_re,
    filter_im,
    weight_re,
    weight_im,
    start_ref,
    table,
    rate,
    doppler2,
    echo_re,
    echo_im,
    gain_re,
    gain_im,
    beam_ref,
    factor_re,
    factor_im,
    x_re,
    x_im,
    y_ref,
    z_ref,
    m_ref,
    tmp_re,
    tmp_im,
    u_ref,
    w_ref,
    g_re,
    g_im,
    q_ref,
    rate_ref,
    part_ref,
    from_sibling,
    summed,
    from_x,
    reduced,
    echo_sems,
    gain_sems,
    sib_send,
    sib_recv,
    x_send,
    x_recv,
    yz_send,
    yz_recv,
    own,
):
    chans, pulses = echo_re.shape[0], echo_re.shape[1]
    chunk_rows = pulses // CHUNKS
    per_chan = chunk_rows // ROWS
    cols = rate.shape[0]
    chan = lax.axis_index("chan")
    x, y, z, core = place()
    mine_yz = y * 4 + z
    sibling = device_at(x, y, z, 1 - core)

    def along_x(offset):
        return device_at((x + offset) % 4, y, z, core)

    def along_yz(offset):
        return (y + offset[0]) % 4, (z + offset[1]) % 4

    barrier = pltpu.get_barrier_semaphore()
    pl.semaphore_signal(barrier, inc=1, device_id=sibling, device_id_type=MESH)
    for offset in X_OFFSETS:
        pl.semaphore_signal(barrier, inc=1, device_id=along_x(offset), device_id_type=MESH)
    for offset in YZ_OFFSETS:
        pl.semaphore_signal(
            barrier, inc=1, device_id=device_at(x, *along_yz(offset), core), device_id_type=MESH
        )

    def echo_copies(i):
        rows = pl.ds(pl.multiple_of(i * chunk_rows, chunk_rows), chunk_rows)
        return (
            pltpu.make_async_copy(echo_re.at[:, rows], x_re.at[:, rows], echo_sems.at[0, i]),
            pltpu.make_async_copy(echo_im.at[:, rows], x_im.at[:, rows], echo_sems.at[1, i]),
        )

    @pl.loop(0, CHUNKS)
    def _(i):
        for copy in echo_copies(i):
            copy.start()

    gain_copies = (
        pltpu.make_async_copy(gain_re, g_re, gain_sems.at[0]),
        pltpu.make_async_copy(gain_im, g_im, gain_sems.at[1]),
    )
    for copy in gain_copies:
        copy.start()

    def hdot(one, two):
        return jnp.dot(one, two, precision=lax.Precision.HIGHEST, preferred_element_type=F32)

    ht_re, ht_im = filter_re[...].T, filter_im[...].T
    c_re = jnp.zeros((OUTER, LANES), F32)
    c_im = jnp.zeros((OUTER, LANES), F32)
    for parity in (0, 1):
        rows = slice(parity * OUTER, (parity + 1) * OUTER)
        t_re, t_im = table[2 * parity], table[2 * parity + 1]
        c_re = c_re + hdot(ht_re[rows], t_re) - hdot(ht_im[rows], t_im)
        c_im = c_im + hdot(ht_re[rows], t_im) + hdot(ht_im[rows], t_re)
    upper = cmul((c_re, c_im), (table[4], table[5]))
    lower = cmul((c_re, c_im), (table[6], table[7]))
    u_ref[0], u_ref[1] = upper
    u_ref[2], u_ref[3] = lower

    @pl.loop(0, OUTER, unroll=4)
    def _(a):
        start = start_ref[a]
        for c in range(chans):
            channel = chan * chans + c
            live = jnp.logical_and(channel >= start, channel < start + ACTIVE).astype(F32)
            lanes = pl.ds(pl.multiple_of(a * LANES, LANES), LANES)
            w_ref[0, c, pl.ds(a, 1), :] = weight_re[c : c + 1, lanes] * live
            w_ref[1, c, pl.ds(a, 1), :] = weight_im[c : c + 1, lanes] * live

    sub_index = lax.broadcasted_iota(jnp.int32, (LANES, LANES), 0)
    lane_index = lax.broadcasted_iota(jnp.int32, (LANES, LANES), 1)
    on_upper = lane_index >= sub_index

    @pl.loop(0, OUTER, unroll=8)
    def _(k):
        def toeplitz(part):
            def rolled(which):
                row = jnp.broadcast_to(u_ref[which, pl.ds(k, 1), :], (LANES, LANES))
                return pltpu.roll(row, 0, 1, stride=1, stride_axis=0)

            return jnp.where(on_upper, rolled(part), rolled(2 + part))

        m_re, m_im = toeplitz(0), toeplitz(1)
        m_ref[k, 0:LANES, 0:LANES] = m_re.astype(BF16)
        m_ref[k, 0:LANES, LANES : 2 * LANES] = m_im.astype(BF16)
        m_ref[k, LANES : 2 * LANES, 0:LANES] = (-m_im).astype(BF16)
        m_ref[k, LANES : 2 * LANES, LANES : 2 * LANES] = m_re.astype(BF16)

    def outer_forward(i):
        for copy in echo_copies(i):
            copy.wait()

        @pl.loop(0, chans * per_chan)
        def _(it):
            c, r = it // per_chan, it % per_chan
            rows = pl.ds(pl.multiple_of(i * chunk_rows + r * ROWS, ROWS), ROWS)
            out_rows = pl.ds(pl.multiple_of(it * ROWS, ROWS), ROWS)

            def load(a):
                lanes = slice(a * LANES, (a + 1) * LANES)
                return (x_re[c, rows, lanes].astype(F32), x_im[c, rows, lanes].astype(F32))

            def store(low, k, value):
                tmp_re[0, low * 8 + k] = value[0]
                tmp_im[0, low * 8 + k] = value[1]

            first_pass(load, store, OUTER, 8, -1)
            for k in range(8):
                part = dft([(tmp_re[0, low * 8 + k], tmp_im[0, low * 8 + k]) for low in range(8)], -1)
                for j, value in enumerate(part):
                    y_ref[k + 8 * j, out_rows, 0:LANES] = value[0].astype(BF16)
                    y_ref[k + 8 * j, out_rows, LANES : 2 * LANES] = value[1].astype(BF16)

    def filter_inner():
        @pl.loop(0, OUTER, unroll=16)
        def _(k):
            z_ref[k] = jnp.dot(y_ref[k], m_ref[k], preferred_element_type=F32)

    low_half = lax.broadcasted_iota(jnp.int32, (ROWS, LANES), 1) < LANES // 2

    def outer_inverse(i):
        @pl.loop(0, per_chan)
        def _(r):
            for c in range(chans):
                in_rows = pl.ds(pl.multiple_of(c * chunk_rows + r * ROWS, ROWS), ROWS)

                def load(k):
                    return (z_ref[k, in_rows, 0:LANES], z_ref[k, in_rows, LANES : 2 * LANES])

                def store(low, k, value):
                    tmp_re[c, low * 8 + k] = value[0]
                    tmp_im[c, low * 8 + k] = value[1]

                first_pass(load, store, OUTER, 8, 1)
            rows = pl.ds(pl.multiple_of(r * ROWS, ROWS), ROWS)
            for k in range(8):
                total = None
                for c in range(chans):
                    part = dft(
                        [(tmp_re[c, low * 8 + k], tmp_im[c, low * 8 + k]) for low in range(8)], 1
                    )
                    weighted = []
                    for j, value in enumerate(part):
                        a = k + 8 * j
                        weight = (w_ref[0, c, a : a + 1, :], w_ref[1, c, a : a + 1, :])
                        weighted.append(cmul(value, weight))
                    total = weighted if total is None else [add(o, t) for o, t in zip(total, weighted)]
                for j, (re, im) in enumerate(total):
                    half = LANES // 2
                    first = jnp.where(low_half, re, pltpu.roll(im, half, 1))
                    second = jnp.where(low_half, pltpu.roll(re, half, 1), im)
                    for side, value in enumerate((first, second)):
                        owner = 2 * (k + 8 * j) + side
                        to_high, to_core, to_pulse = owner // 64, owner // 32 % 2, owner % 32
                        part_ref[i, to_high, to_core, to_pulse, rows, :] = value.astype(BF16)

    def sibling_copy(i, to_high):
        return pltpu.make_async_remote_copy(
            src_ref=part_ref.at[i, to_high, 1 - core],
            dst_ref=from_sibling.at[i, to_high],
            send_sem=sib_send.at[i, to_high],
            recv_sem=sib_recv.at[i, to_high],
            device_id=sibling,
            device_id_type=MESH,
        )

    def x_copy(i, n):
        offset = X_OFFSETS[n]
        return pltpu.make_async_remote_copy(
            src_ref=summed.at[i, (x + offset) % 4],
            dst_ref=from_x.at[i, x],
            send_sem=x_send.at[i, n],
            recv_sem=x_recv.at[i, n],
            device_id=along_x(offset),
            device_id_type=MESH,
        )

    def yz_copy(i, n):
        to_y, to_z = along_yz(YZ_OFFSETS[n])
        return pltpu.make_async_remote_copy(
            src_ref=reduced.at[i, to_y * 4 + to_z],
            dst_ref=beam_ref.at[i, mine_yz],
            send_sem=yz_send.at[i, n],
            recv_sem=yz_recv.at[i, n],
            device_id=device_at(x, to_y, to_z, core),
            device_id_type=MESH,
        )

    def own_x_copy(i):
        return pltpu.make_async_copy(summed.at[i, x], from_x.at[i, x], own.at[0, i])

    def own_yz_copy(i):
        return pltpu.make_async_copy(
            reduced.at[i, mine_yz], beam_ref.at[i, mine_yz], own.at[1, i]
        )

    def send_along_x(i):
        for to_high in range(2):
            sibling_copy(i, to_high).wait_recv()
        for to_x in range(4):

            @pl.loop(0, YZ, unroll=8)
            def _(j):
                block = (to_x % 2) * YZ + j
                total = part_ref[i, to_x // 2, core, block].astype(F32) + from_sibling[
                    i, to_x // 2, block
                ].astype(F32)
                summed[i, to_x, j] = total.astype(BF16)

        for n in range(len(X_OFFSETS)):
            x_copy(i, n).start()
        own_x_copy(i).start()

    def send_along_yz(i):
        for n in range(len(X_OFFSETS)):
            x_copy(i, n).wait_recv()
        own_x_copy(i).wait()

        @pl.loop(0, YZ, unroll=4)
        def _(j):
            for low in range(2):
                total = from_x[i, low, j].astype(F32) + from_x[i, low + 2, j].astype(F32)
                reduced[i, j, low] = total.astype(BF16)

        for n in range(len(YZ_OFFSETS)):
            yz_copy(i, n).start()
        own_yz_copy(i).start()

    def gains_by_row():
        for copy in gain_copies:
            copy.wait()

        @pl.loop(0, AZ_OUTER, unroll=4)
        def _(j):
            lanes = pl.ds(pl.multiple_of(j * LANES, LANES), LANES)
            q_ref[lanes, :] = jnp.concatenate([g_re[:, lanes], g_im[:, lanes]], axis=0).T

        @pl.loop(0, cols, unroll=8)
        def _(n):
            rate_ref[pl.ds(n, 1), :] = jnp.full((1, LANES), rate[n], F32)

    def azimuth_factor():
        @pl.loop(0, AZ_OUTER, unroll=2)
        def _(k):
            gains = q_ref[pl.ds(k, LANES, stride=AZ_OUTER), :].T
            cosine, sine = unit_of_half_turns(rate_ref[...] * doppler2[pl.ds(k, 1), :])
            re, im = gains[0:cols], gains[cols : 2 * cols]
            factor_re[k] = cosine * re + sine * im
            factor_im[k] = cosine * im - sine * re

    pl.semaphore_wait(barrier, 1 + len(X_OFFSETS) + len(YZ_OFFSETS))

    @pl.loop(0, CHUNKS + 1)
    def _(i):
        @pl.when(i < CHUNKS)
        def _():
            outer_forward(i)

        @pl.when(i == CHUNKS)
        def _():
            gains_by_row()

        @pl.when(i > 0)
        def _():
            send_along_x(i - 1)

        @pl.when(i > 2)
        def _():
            send_along_yz(i - 3)

        @pl.when(i < CHUNKS)
        def _():
            filter_inner()
            outer_inverse(i)
            for to_high in range(2):
                sibling_copy(i, to_high).start()

        @pl.when(i == CHUNKS)
        def _():
            azimuth_factor()

    @pl.loop(CHUNKS - 2, CHUNKS)
    def _(i):
        send_along_yz(i)

    @pl.loop(0, CHUNKS)
    def _(i):
        for n in range(len(YZ_OFFSETS)):
            yz_copy(i, n).wait()
        own_yz_copy(i).wait()
        for n in range(len(X_OFFSETS)):
            x_copy(i, n).wait_send()
        for to_high in range(2):
            sibling_copy(i, to_high).wait_send()


def range_call(
    echo_re, echo_im, filter_re, filter_im, weight_re, weight_im, window_start, gain_re, gain_im, rate
):
    chans, pulses, samples = echo_re.shape
    cols = rate.shape[0]
    chunk_rows = pulses // CHUNKS
    vmem = pl.BlockSpec(memory_space=VMEM)
    smem = pl.BlockSpec(memory_space=pltpu.SMEM)
    hbm = pl.BlockSpec(memory_space=pl.ANY)
    dma = pltpu.SemaphoreType.DMA
    factor = VMEM((AZ_OUTER, cols, LANES), F32)
    return pl.pallas_call(
        range_kernel,
        out_shape=(
            VMEM((CHUNKS, YZ, 2, chunk_rows, LANES), BF16),
            factor,
            factor,
        ),
        in_specs=[vmem, vmem, vmem, vmem, smem, vmem, smem, vmem, hbm, hbm, hbm, hbm],
        out_specs=(vmem, vmem, vmem),
        scratch_shapes=[
            VMEM((chans, pulses, samples), BF16),
            VMEM((chans, pulses, samples), BF16),
            VMEM((OUTER, chans * chunk_rows, 2 * LANES), BF16),
            VMEM((OUTER, chans * chunk_rows, 2 * LANES), F32),
            VMEM((OUTER, 2 * LANES, 2 * LANES), BF16),
            VMEM((chans, OUTER, ROWS, LANES), F32),
            VMEM((chans, OUTER, ROWS, LANES), F32),
            VMEM((4, OUTER, LANES), F32),
            VMEM((2, chans, OUTER, LANES), F32),
            VMEM((cols, PULSES), F32),
            VMEM((cols, PULSES), F32),
            VMEM((PULSES, LANES), F32),
            VMEM((cols, LANES), F32),
            VMEM((CHUNKS, 2, 2, AZ_OUTER, chunk_rows, LANES), BF16),
            VMEM((CHUNKS, 2, AZ_OUTER, chunk_rows, LANES), BF16),
            VMEM((CHUNKS, 4, YZ, chunk_rows, LANES), BF16),
            VMEM((CHUNKS, 4, YZ, chunk_rows, LANES), BF16),
            VMEM((CHUNKS, YZ, 2, chunk_rows, LANES), BF16),
            dma((2, CHUNKS)),
            dma((2,)),
            dma((CHUNKS, 2)),
            dma((CHUNKS, 2)),
            dma((CHUNKS, len(X_OFFSETS))),
            dma((CHUNKS, len(X_OFFSETS))),
            dma((CHUNKS, len(YZ_OFFSETS))),
            dma((CHUNKS, len(YZ_OFFSETS))),
            dma((2, CHUNKS)),
        ],
        compiler_params=pltpu.CompilerParams(
            collective_id=0, has_side_effects=True, vmem_limit_bytes=54 * MIB
        ),
        name="range_exchange",
    )(
        filter_re.reshape(OUTER, LANES),
        filter_im.reshape(OUTER, LANES),
        weight_re,
        weight_im,
        window_start,
        jnp.asarray(range_tables()),
        rate,
        jnp.asarray(azimuth_tables()[2][2]),
        echo_re,
        echo_im,
        gain_re,
        gain_im,
    )


GROUP = 4


def split_dot(x, table):
    high = x.astype(BF16)
    low = (x - high.astype(F32)).astype(BF16)
    return jnp.dot(
        jnp.concatenate([high, low, high], axis=1), table, preferred_element_type=F32
    )


def azimuth_kernel(
    beam, factor_re, factor_im, forward, inverse, small, eye, out_re, out_im, a_ref, b_ref, tmp_re, tmp_im
):
    cols = out_re.shape[0]
    twiddle_re, twiddle_im = small.at[0], small.at[1]

    @pl.loop(0, AZ_OUTER, unroll=8)
    def _(s):
        block = jnp.concatenate([beam[i, s % YZ, s // YZ] for i in range(beam.shape[0])], axis=0)
        a_ref[s] = lax.dot_general(
            eye[...], block, (((1,), (1,)), ((), ())), preferred_element_type=F32
        )

    def stash(low, k, value):
        tmp_re[low * 8 + k] = value[0]
        tmp_im[low * 8 + k] = value[1]

    def second(k, sign):
        return dft([(tmp_re[low * 8 + k], tmp_im[low * 8 + k]) for low in range(4)], sign)

    @pl.loop(0, cols // 8)
    def _(r):
        re_rows = pl.ds(pl.multiple_of(r * 8, 8), 8)
        im_rows = pl.ds(pl.multiple_of(cols + r * 8, 8), 8)
        first_pass(lambda s: (a_ref[s, re_rows, :], a_ref[s, im_rows, :]), stash, AZ_OUTER, 4, -1)
        for k in range(8):
            for j, value in enumerate(second(k, -1)):
                at = k + 8 * j
                re, im = cmul(value, (twiddle_re[at : at + 1, :], twiddle_im[at : at + 1, :]))
                b_ref[at, re_rows, 0:LANES] = re
                b_ref[at, re_rows, LANES : 2 * LANES] = im

    @pl.loop(0, AZ_OUTER // GROUP, unroll=2)
    def _(g):
        at = pl.ds(g * GROUP, GROUP)
        x = b_ref[at].reshape(GROUP * cols, 2 * LANES)
        s = split_dot(x, forward[...]).reshape(GROUP, cols, 2 * LANES)
        parts = []
        for i in range(GROUP):
            factor = (factor_re[g * GROUP + i], factor_im[g * GROUP + i])
            re, im = cmul((s[i, :, 0:LANES], s[i, :, LANES : 2 * LANES]), factor)
            parts.append(jnp.concatenate([re, im], axis=1))
        focused = split_dot(jnp.concatenate(parts, axis=0), inverse[...])
        b_ref[at] = focused.reshape(GROUP, cols, 2 * LANES)

    @pl.loop(0, cols // 8)
    def _(r):
        rows = pl.ds(pl.multiple_of(r * 8, 8), 8)

        def load(k):
            value = (b_ref[k, rows, 0:LANES], b_ref[k, rows, LANES : 2 * LANES])
            return cmul(value, (twiddle_re[k : k + 1, :], -twiddle_im[k : k + 1, :]))

        first_pass(load, stash, AZ_OUTER, 4, 1)
        for k in range(8):
            for j, value in enumerate(second(k, 1)):
                s = k + 8 * j
                out_re[rows, s * LANES : (s + 1) * LANES] = value[0]
                out_im[rows, s * LANES : (s + 1) * LANES] = value[1]


def azimuth_call(beam, factor_re, factor_im):
    cols = factor_re.shape[1]
    forward, inverse, small, eye = azimuth_tables()
    shape = jax.ShapeDtypeStruct((cols, PULSES), F32)
    vmem = pl.BlockSpec(memory_space=VMEM)

    return pl.pallas_call(
        azimuth_kernel,
        out_shape=(shape, shape),
        in_specs=[vmem] * 7,
        out_specs=(vmem, vmem),
        scratch_shapes=[
            VMEM((AZ_OUTER, 2 * cols, LANES), F32),
            VMEM((AZ_OUTER, cols, 2 * LANES), F32),
            VMEM((AZ_OUTER, 8, LANES), F32),
            VMEM((AZ_OUTER, 8, LANES), F32),
        ],
        compiler_params=pltpu.CompilerParams(vmem_limit_bytes=32 * MIB),
        name="azimuth_focus",
    )(
        beam,
        factor_re,
        factor_im,
        jnp.asarray(forward),
        jnp.asarray(inverse),
        jnp.asarray(small),
        jnp.asarray(eye),
    )


def local(
    echo_re,
    echo_im,
    range_filter_re,
    range_filter_im,
    beam_weight_re,
    beam_weight_im,
    window_start,
    azimuth_filter_re,
    azimuth_filter_im,
    migration_rate,
):
    beam, factor_re, factor_im = range_call(
        echo_re,
        echo_im,
        range_filter_re,
        range_filter_im,
        beam_weight_re,
        beam_weight_im,
        window_start,
        azimuth_filter_re,
        azimuth_filter_im,
        migration_rate,
    )
    return azimuth_call(beam, factor_re, factor_im)


def solution(mesh):
    placed = (
        P("chan", "pulse", None),
        P("chan", "pulse", None),
        P(),
        P(),
        P("chan", None),
        P("chan", None),
        P(),
        P(("chan", "pulse"), None),
        P(("chan", "pulse"), None),
        P(("chan", "pulse")),
    )
    return jax.shard_map(
        local,
        mesh=mesh,
        in_specs=placed,
        out_specs=(P(("chan", "pulse"), None), P(("chan", "pulse"), None)),
        check_vma=False,
    )
```

```python
import functools
import math

import jax
import jax.numpy as jnp
import numpy as np
from jax import lax
from jax.experimental import pallas as pl
from jax.experimental.pallas import tpu as pltpu
from jax.sharding import PartitionSpec as P

ACTIVE = 4
F32 = jnp.float32
BF16 = jnp.bfloat16
MESH = pl.DeviceIdType.MESH
VMEM = pltpu.VMEM
MIB = 1024 * 1024

OUTER = 64
LANES = 128
RANGE = OUTER * LANES
AZ_OUTER = 32
PULSES = AZ_OUTER * LANES


def unit(numerator, denominator):
    angle = 2.0 * np.pi * (np.asarray(numerator) % denominator) / denominator
    return np.cos(angle), np.sin(angle)


def f32_pair(pair):
    return tuple(np.asarray(part, np.float32) for part in pair)


def range_tables():
    row = np.arange(OUTER)[:, None]
    lane = np.arange(LANES)[None, :]
    tables = []
    for parity in (0, 1):
        re, im = unit(lane * (2 * row + parity), LANES)
        tables += f32_pair((re / RANGE, im / RANGE))
    tables += f32_pair(unit(row * lane, RANGE))
    tables += f32_pair(unit(row * (lane - LANES), RANGE))
    return np.stack(tables)


def real_form(pair):
    re, im = pair
    return np.block([[re, im], [-im, re]])


def split_table(table):
    high = table.astype(BF16)
    low = (table - high.astype(np.float64)).astype(BF16)
    return np.concatenate([high, high, low], axis=0)


def azimuth_tables():
    index = np.arange(LANES)
    row = np.arange(AZ_OUTER)[:, None]
    lane = index[None, :]
    grid = index[:, None] * index[None, :]
    forward = split_table(real_form(unit(-grid, LANES)))
    inverse = split_table(real_form(unit(grid, LANES)) / PULSES)
    twiddle_re, twiddle_im = unit(-row * lane, PULSES)
    frequency = row + AZ_OUTER * lane
    doppler = ((frequency + PULSES // 2) % PULSES - PULSES // 2) * (2.0 / PULSES)
    small = np.stack(f32_pair((twiddle_re, twiddle_im)) + (np.asarray(doppler**2, np.float32),))
    eye = np.eye(LANES).astype(BF16)
    return forward, inverse, small, eye


def times(value, numerator, denominator):
    re, im = value
    eighth = (numerator * 8) / denominator % 8
    if eighth == 0:
        return value
    if eighth == 2:
        return (-im, re)
    if eighth == 4:
        return (-re, -im)
    if eighth == 6:
        return (im, -re)
    half = math.sqrt(0.5)
    if eighth == 1:
        return ((re - im) * half, (re + im) * half)
    if eighth == 3:
        return ((re + im) * -half, (re - im) * half)
    if eighth == 5:
        return ((im - re) * half, (re + im) * -half)
    if eighth == 7:
        return ((re + im) * half, (im - re) * half)
    cosine = math.cos(2.0 * math.pi * numerator / denominator)
    sine = math.sin(2.0 * math.pi * numerator / denominator)
    return (re * cosine - im * sine, re * sine + im * cosine)


def add(one, two):
    return (one[0] + two[0], one[1] + two[1])


def sub(one, two):
    return (one[0] - two[0], one[1] - two[1])


def dft(values, sign):
    count = len(values)
    if count == 1:
        return values
    even = dft(values[0::2], sign)
    odd = dft(values[1::2], sign)
    odd = [times(value, sign * k, count) for k, value in enumerate(odd)]
    return [add(e, o) for e, o in zip(even, odd)] + [sub(e, o) for e, o in zip(even, odd)]


def cmul(one, two):
    return (one[0] * two[0] - one[1] * two[1], one[0] * two[1] + one[1] * two[0])


def first_pass(load, store, count, fine, sign):
    high = count // fine
    for low in range(fine):
        part = dft([load(fine * j + low) for j in range(high)], sign)
        for k, value in enumerate(part):
            store(low, k, times(value, sign * low * k, count))


def unit_of_half_turns(turns):
    quarter = jnp.floor(turns * 2.0 + 0.5)
    x = (turns - quarter * 0.5) * math.pi
    y = x * x
    sine = x * (1.0 + y * (-1.0 / 6 + y * (1.0 / 120 + y * (-1.0 / 5040 + y * (1.0 / 362880)))))
    cosine = 1.0 + y * (-0.5 + y * (1.0 / 24 + y * (-1.0 / 720 + y * (1.0 / 40320))))
    index = quarter.astype(jnp.int32)
    swap = index % 2 == 1
    one = jnp.where(swap, sine, cosine)
    two = jnp.where(swap, cosine, sine)
    one = jnp.where((index + 1) // 2 % 2 == 1, -one, one)
    two = jnp.where(index // 2 % 2 == 1, -two, two)
    return one, two


ROWS = 16
CHUNKS = 8
PARTS = 2
PART_CHUNKS = CHUNKS // PARTS
X_OFFSETS = (2, 1, 3)
YZ_OFFSETS = sorted(
    [(y, z) for y in range(4) for z in range(4) if (y, z) != (0, 0)],
    key=lambda offset: -sum(min(d, 4 - d) for d in offset),
)
YZ = 16
OFFSETS = sorted(
    [(x, y, z) for x in range(4) for y in range(4) for z in range(4) if (x, y, z) != (0, 0, 0)],
    key=lambda offset: -sum(min(d, 4 - d) for d in offset),
)


def place():
    chan, pulse = lax.axis_index("chan"), lax.axis_index("pulse")
    return (chan // 2) * 2 + pulse // 16, (pulse // 4) % 4, pulse % 4, chan % 2


def device_at(x, y, z, core):
    return ((x // 2) * 2 + core, (x % 2) * 16 + y * 4 + z)


def range_kernel(
    filter_re,
    filter_im,
    weight_re,
    weight_im,
    start_ref,
    table,
    rate,
    doppler2,
    echo_re,
    echo_im,
    gain_re,
    gain_im,
    beam_ref,
    last_ref,
    factor_re,
    factor_im,
    x_re,
    x_im,
    y_ref,
    z_ref,
    m_ref,
    tmp_re,
    tmp_im,
    u_ref,
    w_ref,
    g_re,
    g_im,
    q_ref,
    rate_ref,
    part_ref,
    from_sibling,
    summed,
    from_x,
    reduced,
    echo_sems,
    gain_sems,
    sib_send,
    sib_recv,
    x_send,
    x_recv,
    yz_send,
    yz_recv,
    last_send,
    last_recv,
    own,
):
    chans, pulses = echo_re.shape[0], echo_re.shape[1]
    part_rows = PART_CHUNKS * ROWS
    cols = rate.shape[0]
    chan = lax.axis_index("chan")
    x, y, z, core = place()
    mine_yz = y * 4 + z
    sibling = device_at(x, y, z, 1 - core)

    def along_x(offset):
        return device_at((x + offset) % 4, y, z, core)

    def along_yz(offset):
        return (y + offset[0]) % 4, (z + offset[1]) % 4

    def anywhere(offset):
        return (x + offset[0]) % 4, (y + offset[1]) % 4, (z + offset[2]) % 4

    def echo_copies(i):
        rows = pl.ds(pl.multiple_of(i * ROWS, ROWS), ROWS)
        return (
            pltpu.make_async_copy(echo_re.at[:, rows], x_re.at[:, rows], echo_sems.at[0, i]),
            pltpu.make_async_copy(echo_im.at[:, rows], x_im.at[:, rows], echo_sems.at[1, i]),
        )

    @pl.loop(0, CHUNKS)
    def _(i):
        for copy in echo_copies(i):
            copy.start()

    gain_copies = (
        pltpu.make_async_copy(gain_re, g_re, gain_sems.at[0]),
        pltpu.make_async_copy(gain_im, g_im, gain_sems.at[1]),
    )
    for copy in gain_copies:
        copy.start()

    barrier = pltpu.get_barrier_semaphore()
    pl.semaphore_signal(barrier, inc=1, device_id=sibling, device_id_type=MESH)
    for offset in OFFSETS:
        pl.semaphore_signal(
            barrier, inc=1, device_id=device_at(*anywhere(offset), core), device_id_type=MESH
        )

    def hdot(one, two):
        return jnp.dot(one, two, precision=lax.Precision.HIGHEST, preferred_element_type=F32)

    ht_re, ht_im = filter_re[...].T, filter_im[...].T
    c_re = jnp.zeros((OUTER, LANES), F32)
    c_im = jnp.zeros((OUTER, LANES), F32)
    for parity in (0, 1):
        rows = slice(parity * OUTER, (parity + 1) * OUTER)
        t_re, t_im = table[2 * parity], table[2 * parity + 1]
        c_re = c_re + hdot(ht_re[rows], t_re) - hdot(ht_im[rows], t_im)
        c_im = c_im + hdot(ht_re[rows], t_im) + hdot(ht_im[rows], t_re)
    upper = cmul((c_re, c_im), (table[4], table[5]))
    lower = cmul((c_re, c_im), (table[6], table[7]))
    u_ref[0], u_ref[1] = upper
    u_ref[2], u_ref[3] = lower

    @pl.loop(0, OUTER, unroll=4)
    def _(a):
        start = start_ref[a]
        for c in range(chans):
            channel = chan * chans + c
            live = jnp.logical_and(channel >= start, channel < start + ACTIVE).astype(F32)
            lanes = pl.ds(pl.multiple_of(a * LANES, LANES), LANES)
            w_ref[0, c, pl.ds(a, 1), :] = weight_re[c : c + 1, lanes] * live
            w_ref[1, c, pl.ds(a, 1), :] = weight_im[c : c + 1, lanes] * live

    sub_index = lax.broadcasted_iota(jnp.int32, (LANES, LANES), 0)
    lane_index = lax.broadcasted_iota(jnp.int32, (LANES, LANES), 1)
    on_upper = lane_index >= sub_index

    def build_matrix(k):
        def toeplitz(part):
            def rolled(which):
                row = jnp.broadcast_to(u_ref[which, pl.ds(k, 1), :], (LANES, LANES))
                return pltpu.roll(row, 0, 1, stride=1, stride_axis=0)

            return jnp.where(on_upper, rolled(part), rolled(2 + part))

        m_re, m_im = toeplitz(0), toeplitz(1)
        m_ref[k, 0:LANES, 0:LANES] = m_re.astype(BF16)
        m_ref[k, 0:LANES, LANES : 2 * LANES] = m_im.astype(BF16)
        m_ref[k, LANES : 2 * LANES, 0:LANES] = (-m_im).astype(BF16)
        m_ref[k, LANES : 2 * LANES, LANES : 2 * LANES] = m_re.astype(BF16)

    @pl.loop(0, OUTER, unroll=8)
    def _(k):
        build_matrix(k)

    def outer_forward(h):
        first = h * PART_CHUNKS

        @pl.loop(0, chans * PART_CHUNKS)
        def _(it):
            r, c = it // chans, it % chans

            @pl.when(c == 0)
            def _():
                for copy in echo_copies(first + r):
                    copy.wait()

            rows = pl.ds(pl.multiple_of((first + r) * ROWS, ROWS), ROWS)
            out_rows = pl.ds(pl.multiple_of(c * part_rows + r * ROWS, ROWS), ROWS)

            def load(a):
                lanes = slice(a * LANES, (a + 1) * LANES)
                return (x_re[c, rows, lanes].astype(F32), x_im[c, rows, lanes].astype(F32))

            def store(low, k, value):
                tmp_re[0, low * 8 + k] = value[0]
                tmp_im[0, low * 8 + k] = value[1]

            first_pass(load, store, OUTER, 8, -1)
            for k in range(8):
                part = dft([(tmp_re[0, low * 8 + k], tmp_im[0, low * 8 + k]) for low in range(8)], -1)
                for j, value in enumerate(part):
                    y_ref[k + 8 * j, out_rows, 0:LANES] = value[0].astype(BF16)
                    y_ref[k + 8 * j, out_rows, LANES : 2 * LANES] = value[1].astype(BF16)

    def filter_inner():
        @pl.loop(0, OUTER, unroll=16)
        def _(k):
            z_ref[k] = jnp.dot(y_ref[k], m_ref[k], preferred_element_type=F32)

    low_half = lax.broadcasted_iota(jnp.int32, (ROWS, LANES), 1) < LANES // 2

    def outer_inverse(i, j):
        for c in range(chans):
            in_rows = pl.ds(pl.multiple_of(c * part_rows + j * ROWS, ROWS), ROWS)

            def load(k):
                return (z_ref[k, in_rows, 0:LANES], z_ref[k, in_rows, LANES : 2 * LANES])

            def store(low, k, value):
                tmp_re[c, low * 8 + k] = value[0]
                tmp_im[c, low * 8 + k] = value[1]

            first_pass(load, store, OUTER, 8, 1)
        for k in range(8):
            total = None
            for c in range(chans):
                part = dft(
                    [(tmp_re[c, low * 8 + k], tmp_im[c, low * 8 + k]) for low in range(8)], 1
                )
                weighted = []
                for j, value in enumerate(part):
                    a = k + 8 * j
                    weight = (w_ref[0, c, a : a + 1, :], w_ref[1, c, a : a + 1, :])
                    weighted.append(cmul(value, weight))
                total = weighted if total is None else [add(o, t) for o, t in zip(total, weighted)]
            for j, (re, im) in enumerate(total):
                half = LANES // 2
                first = jnp.where(low_half, re, pltpu.roll(im, half, 1))
                second = jnp.where(low_half, pltpu.roll(re, half, 1), im)
                for side, value in enumerate((first, second)):
                    owner = 2 * (k + 8 * j) + side
                    to_high, to_core, to_pulse = owner // 64, owner // 32 % 2, owner % 32
                    part_ref[i, to_high, to_core, to_pulse] = value.astype(BF16)

    def sibling_copy(i, to_high):
        return pltpu.make_async_remote_copy(
            src_ref=part_ref.at[i, to_high, 1 - core],
            dst_ref=from_sibling.at[i, to_high],
            send_sem=sib_send.at[i, to_high],
            recv_sem=sib_recv.at[i, to_high],
            device_id=sibling,
            device_id_type=MESH,
        )

    def x_copy(i, n):
        offset = X_OFFSETS[n]
        return pltpu.make_async_remote_copy(
            src_ref=summed.at[i, (x + offset) % 4],
            dst_ref=from_x.at[i, x],
            send_sem=x_send.at[i, n],
            recv_sem=x_recv.at[i, n],
            device_id=along_x(offset),
            device_id_type=MESH,
        )

    def yz_copy(i, n):
        to_y, to_z = along_yz(YZ_OFFSETS[n])
        return pltpu.make_async_remote_copy(
            src_ref=reduced.at[i, to_y * 4 + to_z],
            dst_ref=beam_ref.at[i, mine_yz],
            send_sem=yz_send.at[i, n],
            recv_sem=yz_recv.at[i, n],
            device_id=device_at(x, to_y, to_z, core),
            device_id_type=MESH,
        )

    def own_x_copy(i):
        return pltpu.make_async_copy(summed.at[i, x], from_x.at[i, x], own.at[0, i])

    def own_yz_copy(i):
        return pltpu.make_async_copy(
            reduced.at[i, mine_yz], beam_ref.at[i, mine_yz], own.at[1, i]
        )

    def sum_siblings(i):
        for to_high in range(2):
            sibling_copy(i, to_high).wait_recv()
        for to_x in range(4):

            @pl.loop(0, YZ, unroll=8)
            def _(j):
                block = (to_x % 2) * YZ + j
                total = part_ref[i, to_x // 2, core, block].astype(F32) + from_sibling[
                    i, to_x // 2, block
                ].astype(F32)
                summed[i, to_x, j] = total.astype(BF16)

    def send_along_x(i):
        sum_siblings(i)
        for n in range(len(X_OFFSETS)):
            x_copy(i, n).start()
        own_x_copy(i).start()

    def send_along_yz(i):
        for n in range(len(X_OFFSETS)):
            x_copy(i, n).wait_recv()
        own_x_copy(i).wait()

        @pl.loop(0, YZ, unroll=4)
        def _(j):
            for low in range(2):
                total = from_x[i, low, j].astype(F32) + from_x[i, low + 2, j].astype(F32)
                reduced[i, j, low] = total.astype(BF16)

        for n in range(len(YZ_OFFSETS)):
            yz_copy(i, n).start()
        own_yz_copy(i).start()

    def direct_copy(n):
        to_x, to_y, to_z = anywhere(OFFSETS[n])
        return pltpu.make_async_remote_copy(
            src_ref=summed.at[CHUNKS - 1, to_x, to_y * 4 + to_z],
            dst_ref=last_ref.at[x, mine_yz],
            send_sem=last_send.at[n],
            recv_sem=last_recv.at[n],
            device_id=device_at(to_x, to_y, to_z, core),
            device_id_type=MESH,
        )

    def own_last_copy():
        return pltpu.make_async_copy(
            summed.at[CHUNKS - 1, x, mine_yz], last_ref.at[x, mine_yz], own.at[0, CHUNKS - 1]
        )

    def gains_by_row():
        for copy in gain_copies:
            copy.wait()

        @pl.loop(0, AZ_OUTER, unroll=4)
        def _(j):
            lanes = pl.ds(pl.multiple_of(j * LANES, LANES), LANES)
            q_ref[lanes, :] = jnp.concatenate([g_re[:, lanes], g_im[:, lanes]], axis=0).T

        @pl.loop(0, cols, unroll=8)
        def _(n):
            rate_ref[pl.ds(n, 1), :] = jnp.full((1, LANES), rate[n], F32)

    pieces = 4

    def azimuth_factor(piece):
        each = AZ_OUTER // pieces

        @pl.loop(0, each, unroll=2)
        def _(j):
            k = piece * each + j
            gains = q_ref[pl.ds(k, LANES, stride=AZ_OUTER), :].T
            cosine, sine = unit_of_half_turns(rate_ref[...] * doppler2[pl.ds(k, 1), :])
            re, im = gains[0:cols], gains[cols : 2 * cols]
            factor_re[k] = cosine * re + sine * im
            factor_im[k] = cosine * im - sine * re

    pl.semaphore_wait(barrier, 1 + len(OFFSETS))

    @pl.loop(0, PARTS)
    def _(h):
        outer_forward(h)
        first = h * PART_CHUNKS

        @pl.when(h > 0)
        def _():
            send_along_x(first - 1)

        filter_inner()

        @pl.loop(0, PART_CHUNKS)
        def _(j):
            i = first + j
            outer_inverse(i, j)
            for to_high in range(2):
                sibling_copy(i, to_high).start()

            @pl.when(j > 0)
            def _():
                send_along_x(i - 1)

            @pl.when(i >= 4)
            def _():
                send_along_yz(i - 4)

    gains_by_row()
    sum_siblings(CHUNKS - 1)
    for n in range(len(OFFSETS)):
        direct_copy(n).start()
    own_last_copy().start()

    @pl.loop(0, PART_CHUNKS - 1)
    def _(j):
        send_along_yz(PART_CHUNKS + j)
        azimuth_factor(j)

    azimuth_factor(pieces - 1)

    @pl.loop(0, CHUNKS - 1)
    def _(i):
        for n in range(len(YZ_OFFSETS)):
            yz_copy(i, n).wait()
        own_yz_copy(i).wait()
        for n in range(len(X_OFFSETS)):
            x_copy(i, n).wait_send()

    @pl.loop(0, CHUNKS)
    def _(i):
        for to_high in range(2):
            sibling_copy(i, to_high).wait_send()

    for n in range(len(OFFSETS)):
        direct_copy(n).wait()
    own_last_copy().wait()


def range_call(
    echo_re, echo_im, filter_re, filter_im, weight_re, weight_im, window_start, gain_re, gain_im, rate
):
    chans, pulses, samples = echo_re.shape
    cols = rate.shape[0]
    chunk_rows = ROWS
    vmem = pl.BlockSpec(memory_space=VMEM)
    smem = pl.BlockSpec(memory_space=pltpu.SMEM)
    hbm = pl.BlockSpec(memory_space=pl.ANY)
    dma = pltpu.SemaphoreType.DMA
    factor = VMEM((AZ_OUTER, cols, LANES), F32)
    return pl.pallas_call(
        range_kernel,
        out_shape=(
            VMEM((CHUNKS - 1, YZ, 2, chunk_rows, LANES), BF16),
            VMEM((4, YZ, chunk_rows, LANES), BF16),
            factor,
            factor,
        ),
        in_specs=[vmem, vmem, vmem, vmem, smem, vmem, smem, vmem, hbm, hbm, hbm, hbm],
        out_specs=(vmem, vmem, vmem, vmem),
        scratch_shapes=[
            VMEM((chans, pulses, samples), BF16),
            VMEM((chans, pulses, samples), BF16),
            VMEM((OUTER, chans * PART_CHUNKS * ROWS, 2 * LANES), BF16),
            VMEM((OUTER, chans * PART_CHUNKS * ROWS, 2 * LANES), F32),
            VMEM((OUTER, 2 * LANES, 2 * LANES), BF16),
            VMEM((chans, OUTER, ROWS, LANES), F32),
            VMEM((chans, OUTER, ROWS, LANES), F32),
            VMEM((4, OUTER, LANES), F32),
            VMEM((2, chans, OUTER, LANES), F32),
            VMEM((cols, PULSES), F32),
            VMEM((cols, PULSES), F32),
            VMEM((PULSES, LANES), F32),
            VMEM((cols, LANES), F32),
            VMEM((CHUNKS, 2, 2, AZ_OUTER, chunk_rows, LANES), BF16),
            VMEM((CHUNKS, 2, AZ_OUTER, chunk_rows, LANES), BF16),
            VMEM((CHUNKS, 4, YZ, chunk_rows, LANES), BF16),
            VMEM((CHUNKS, 4, YZ, chunk_rows, LANES), BF16),
            VMEM((CHUNKS, YZ, 2, chunk_rows, LANES), BF16),
            dma((2, CHUNKS)),
            dma((2,)),
            dma((CHUNKS, 2)),
            dma((CHUNKS, 2)),
            dma((CHUNKS, len(X_OFFSETS))),
            dma((CHUNKS, len(X_OFFSETS))),
            dma((CHUNKS, len(YZ_OFFSETS))),
            dma((CHUNKS, len(YZ_OFFSETS))),
            dma((len(OFFSETS),)),
            dma((len(OFFSETS),)),
            dma((2, CHUNKS)),
        ],
        compiler_params=pltpu.CompilerParams(
            collective_id=0, has_side_effects=True, vmem_limit_bytes=54 * MIB
        ),
        name="range_exchange",
    )(
        filter_re.reshape(OUTER, LANES),
        filter_im.reshape(OUTER, LANES),
        weight_re,
        weight_im,
        window_start,
        jnp.asarray(range_tables()),
        rate,
        jnp.asarray(azimuth_tables()[2][2]),
        echo_re,
        echo_im,
        gain_re,
        gain_im,
    )


GROUP = 4


def split_dot(x, table):
    high = x.astype(BF16)
    low = (x - high.astype(F32)).astype(BF16)
    return jnp.dot(
        jnp.concatenate([high, low, high], axis=1), table, preferred_element_type=F32
    )


def azimuth_kernel(
    beam, last, factor_re, factor_im, forward, inverse, small, eye, out_re, out_im, a_ref, b_ref, tmp_re, tmp_im
):
    cols = out_re.shape[0]
    twiddle_re, twiddle_im = small.at[0], small.at[1]

    @pl.loop(0, AZ_OUTER, unroll=8)
    def _(s):
        yz, low = s % YZ, s // YZ
        blocks = [beam[i, yz, low] for i in range(beam.shape[0])]
        blocks.append((last[low, yz].astype(F32) + last[low + 2, yz].astype(F32)).astype(BF16))
        block = jnp.concatenate(blocks, axis=0)
        a_ref[s] = lax.dot_general(
            eye[...], block, (((1,), (1,)), ((), ())), preferred_element_type=F32
        )

    def stash(low, k, value):
        tmp_re[low * 8 + k] = value[0]
        tmp_im[low * 8 + k] = value[1]

    def second(k, sign):
        return dft([(tmp_re[low * 8 + k], tmp_im[low * 8 + k]) for low in range(4)], sign)

    @pl.loop(0, cols // 8)
    def _(r):
        re_rows = pl.ds(pl.multiple_of(r * 8, 8), 8)
        im_rows = pl.ds(pl.multiple_of(cols + r * 8, 8), 8)
        first_pass(lambda s: (a_ref[s, re_rows, :], a_ref[s, im_rows, :]), stash, AZ_OUTER, 4, -1)
        for k in range(8):
            for j, value in enumerate(second(k, -1)):
                at = k + 8 * j
                re, im = cmul(value, (twiddle_re[at : at + 1, :], twiddle_im[at : at + 1, :]))
                b_ref[at, re_rows, 0:LANES] = re
                b_ref[at, re_rows, LANES : 2 * LANES] = im

    @pl.loop(0, AZ_OUTER // GROUP, unroll=4)
    def _(g):
        at = pl.ds(g * GROUP, GROUP)
        x = b_ref[at].reshape(GROUP * cols, 2 * LANES)
        s = split_dot(x, forward[...]).reshape(GROUP, cols, 2 * LANES)
        parts = []
        for i in range(GROUP):
            factor = (factor_re[g * GROUP + i], factor_im[g * GROUP + i])
            re, im = cmul((s[i, :, 0:LANES], s[i, :, LANES : 2 * LANES]), factor)
            parts.append(jnp.concatenate([re, im], axis=1))
        focused = split_dot(jnp.concatenate(parts, axis=0), inverse[...])
        b_ref[at] = focused.reshape(GROUP, cols, 2 * LANES)

    @pl.loop(0, cols // 8)
    def _(r):
        rows = pl.ds(pl.multiple_of(r * 8, 8), 8)

        def load(k):
            value = (b_ref[k, rows, 0:LANES], b_ref[k, rows, LANES : 2 * LANES])
            return cmul(value, (twiddle_re[k : k + 1, :], -twiddle_im[k : k + 1, :]))

        first_pass(load, stash, AZ_OUTER, 4, 1)
        for k in range(8):
            for j, value in enumerate(second(k, 1)):
                s = k + 8 * j
                out_re[rows, s * LANES : (s + 1) * LANES] = value[0]
                out_im[rows, s * LANES : (s + 1) * LANES] = value[1]


def azimuth_call(beam, last, factor_re, factor_im):
    cols = factor_re.shape[1]
    forward, inverse, small, eye = azimuth_tables()
    shape = jax.ShapeDtypeStruct((cols, PULSES), F32)
    vmem = pl.BlockSpec(memory_space=VMEM)

    return pl.pallas_call(
        azimuth_kernel,
        out_shape=(shape, shape),
        in_specs=[vmem] * 8,
        out_specs=(vmem, vmem),
        scratch_shapes=[
            VMEM((AZ_OUTER, 2 * cols, LANES), F32),
            VMEM((AZ_OUTER, cols, 2 * LANES), F32),
            VMEM((AZ_OUTER, 8, LANES), F32),
            VMEM((AZ_OUTER, 8, LANES), F32),
        ],
        compiler_params=pltpu.CompilerParams(vmem_limit_bytes=32 * MIB),
        name="azimuth_focus",
    )(
        beam,
        last,
        factor_re,
        factor_im,
        jnp.asarray(forward),
        jnp.asarray(inverse),
        jnp.asarray(small),
        jnp.asarray(eye),
    )


def local(
    echo_re,
    echo_im,
    range_filter_re,
    range_filter_im,
    beam_weight_re,
    beam_weight_im,
    window_start,
    azimuth_filter_re,
    azimuth_filter_im,
    migration_rate,
):
    beam, last, factor_re, factor_im = range_call(
        echo_re,
        echo_im,
        range_filter_re,
        range_filter_im,
        beam_weight_re,
        beam_weight_im,
        window_start,
        azimuth_filter_re,
        azimuth_filter_im,
        migration_rate,
    )
    return azimuth_call(beam, last, factor_re, factor_im)


def solution(mesh):
    placed = (
        P("chan", "pulse", None),
        P("chan", "pulse", None),
        P(),
        P(),
        P("chan", None),
        P("chan", None),
        P(),
        P(("chan", "pulse"), None),
        P(("chan", "pulse"), None),
        P(("chan", "pulse")),
    )
    return jax.shard_map(
        local,
        mesh=mesh,
        in_specs=placed,
        out_specs=(P(("chan", "pulse"), None), P(("chan", "pulse"), None)),
        check_vma=False,
    )
```

```python
import functools
import math

import jax
import jax.numpy as jnp
import numpy as np
from jax import lax
from jax.experimental import pallas as pl
from jax.experimental.pallas import tpu as pltpu
from jax.sharding import PartitionSpec as P

ACTIVE = 4
F32 = jnp.float32
BF16 = jnp.bfloat16
MESH = pl.DeviceIdType.MESH
VMEM = pltpu.VMEM
MIB = 1024 * 1024

OUTER = 64
LANES = 128
RANGE = OUTER * LANES
AZ_OUTER = 32
PULSES = AZ_OUTER * LANES


def unit(numerator, denominator):
    angle = 2.0 * np.pi * (np.asarray(numerator) % denominator) / denominator
    return np.cos(angle), np.sin(angle)


def f32_pair(pair):
    return tuple(np.asarray(part, np.float32) for part in pair)


def range_tables():
    row = np.arange(OUTER)[:, None]
    lane = np.arange(LANES)[None, :]
    tables = []
    for parity in (0, 1):
        re, im = unit(lane * (2 * row + parity), LANES)
        tables += f32_pair((re / RANGE, im / RANGE))
    tables += f32_pair(unit(row * lane, RANGE))
    tables += f32_pair(unit(row * (lane - LANES), RANGE))
    return np.stack(tables)


def real_form(pair):
    re, im = pair
    return np.block([[re, im], [-im, re]])


def split_table(table):
    high = table.astype(BF16)
    return np.concatenate([high, high], axis=0)


def azimuth_tables():
    index = np.arange(LANES)
    row = np.arange(AZ_OUTER)[:, None]
    lane = index[None, :]
    grid = index[:, None] * index[None, :]
    forward = split_table(real_form(unit(-grid, LANES)))
    inverse = split_table(real_form(unit(grid, LANES)) / PULSES)
    twiddle_re, twiddle_im = unit(-row * lane, PULSES)
    frequency = row + AZ_OUTER * lane
    doppler = ((frequency + PULSES // 2) % PULSES - PULSES // 2) * (2.0 / PULSES)
    small = np.stack(f32_pair((twiddle_re, twiddle_im)) + (np.asarray(doppler**2, np.float32),))
    eye = np.eye(LANES).astype(BF16)
    return forward, inverse, small, eye


def times(value, numerator, denominator):
    re, im = value
    eighth = (numerator * 8) / denominator % 8
    if eighth == 0:
        return value
    if eighth == 2:
        return (-im, re)
    if eighth == 4:
        return (-re, -im)
    if eighth == 6:
        return (im, -re)
    half = math.sqrt(0.5)
    if eighth == 1:
        return ((re - im) * half, (re + im) * half)
    if eighth == 3:
        return ((re + im) * -half, (re - im) * half)
    if eighth == 5:
        return ((im - re) * half, (re + im) * -half)
    if eighth == 7:
        return ((re + im) * half, (im - re) * half)
    cosine = math.cos(2.0 * math.pi * numerator / denominator)
    sine = math.sin(2.0 * math.pi * numerator / denominator)
    return (re * cosine - im * sine, re * sine + im * cosine)


def add(one, two):
    return (one[0] + two[0], one[1] + two[1])


def sub(one, two):
    return (one[0] - two[0], one[1] - two[1])


def dft(values, sign):
    count = len(values)
    if count == 1:
        return values
    even = dft(values[0::2], sign)
    odd = dft(values[1::2], sign)
    odd = [times(value, sign * k, count) for k, value in enumerate(odd)]
    return [add(e, o) for e, o in zip(even, odd)] + [sub(e, o) for e, o in zip(even, odd)]


def cmul(one, two):
    return (one[0] * two[0] - one[1] * two[1], one[0] * two[1] + one[1] * two[0])


def first_pass(load, store, count, fine, sign):
    high = count // fine
    for low in range(fine):
        part = dft([load(fine * j + low) for j in range(high)], sign)
        for k, value in enumerate(part):
            store(low, k, times(value, sign * low * k, count))


def unit_of_half_turns(turns):
    quarter = jnp.floor(turns * 2.0 + 0.5)
    x = (turns - quarter * 0.5) * math.pi
    y = x * x
    sine = x * (1.0 + y * (-1.0 / 6 + y * (1.0 / 120 + y * (-1.0 / 5040 + y * (1.0 / 362880)))))
    cosine = 1.0 + y * (-0.5 + y * (1.0 / 24 + y * (-1.0 / 720 + y * (1.0 / 40320))))
    index = quarter.astype(jnp.int32)
    swap = index % 2 == 1
    one = jnp.where(swap, sine, cosine)
    two = jnp.where(swap, cosine, sine)
    one = jnp.where((index + 1) // 2 % 2 == 1, -one, one)
    two = jnp.where(index // 2 % 2 == 1, -two, two)
    return one, two


ROWS = 16
CHUNKS = 8
PARTS = 2
PART_CHUNKS = CHUNKS // PARTS
X_OFFSETS = (2, 1, 3)
YZ_OFFSETS = sorted(
    [(y, z) for y in range(4) for z in range(4) if (y, z) != (0, 0)],
    key=lambda offset: -sum(min(d, 4 - d) for d in offset),
)
YZ = 16
OFFSETS = sorted(
    [(x, y, z) for x in range(4) for y in range(4) for z in range(4) if (x, y, z) != (0, 0, 0)],
    key=lambda offset: -sum(min(d, 4 - d) for d in offset),
)


def place():
    chan, pulse = lax.axis_index("chan"), lax.axis_index("pulse")
    return (chan // 2) * 2 + pulse // 16, (pulse // 4) % 4, pulse % 4, chan % 2


def device_at(x, y, z, core):
    return ((x // 2) * 2 + core, (x % 2) * 16 + y * 4 + z)


def range_kernel(
    filter_re,
    filter_im,
    weight_re,
    weight_im,
    start_ref,
    table,
    rate,
    doppler2,
    echo_re,
    echo_im,
    gain_re,
    gain_im,
    beam_ref,
    last_ref,
    factor_re,
    factor_im,
    x_re,
    x_im,
    y_ref,
    z_ref,
    m_ref,
    tmp_re,
    tmp_im,
    u_ref,
    w_ref,
    g_re,
    g_im,
    q_ref,
    rate_ref,
    part_ref,
    from_sibling,
    summed,
    from_x,
    reduced,
    echo_sems,
    gain_sems,
    sib_send,
    sib_recv,
    x_send,
    x_recv,
    yz_send,
    yz_recv,
    last_send,
    last_recv,
    own,
):
    chans, pulses = echo_re.shape[0], echo_re.shape[1]
    part_rows = PART_CHUNKS * ROWS
    cols = rate.shape[0]
    chan = lax.axis_index("chan")
    x, y, z, core = place()
    mine_yz = y * 4 + z
    sibling = device_at(x, y, z, 1 - core)

    def along_x(offset):
        return device_at((x + offset) % 4, y, z, core)

    def along_yz(offset):
        return (y + offset[0]) % 4, (z + offset[1]) % 4

    def anywhere(offset):
        return (x + offset[0]) % 4, (y + offset[1]) % 4, (z + offset[2]) % 4

    def echo_copies(i):
        rows = pl.ds(pl.multiple_of(i * ROWS, ROWS), ROWS)
        return (
            pltpu.make_async_copy(echo_re.at[:, rows], x_re.at[:, rows], echo_sems.at[0, i]),
            pltpu.make_async_copy(echo_im.at[:, rows], x_im.at[:, rows], echo_sems.at[1, i]),
        )

    @pl.loop(0, CHUNKS)
    def _(i):
        for copy in echo_copies(i):
            copy.start()

    gain_copies = (
        pltpu.make_async_copy(gain_re, g_re, gain_sems.at[0]),
        pltpu.make_async_copy(gain_im, g_im, gain_sems.at[1]),
    )
    for copy in gain_copies:
        copy.start()

    barrier = pltpu.get_barrier_semaphore()
    pl.semaphore_signal(barrier, inc=1, device_id=sibling, device_id_type=MESH)
    for offset in OFFSETS:
        pl.semaphore_signal(
            barrier, inc=1, device_id=device_at(*anywhere(offset), core), device_id_type=MESH
        )

    def hdot(one, two):
        return jnp.dot(one, two, precision=lax.Precision.HIGHEST, preferred_element_type=F32)

    ht_re, ht_im = filter_re[...].T, filter_im[...].T
    c_re = jnp.zeros((OUTER, LANES), F32)
    c_im = jnp.zeros((OUTER, LANES), F32)
    for parity in (0, 1):
        rows = slice(parity * OUTER, (parity + 1) * OUTER)
        t_re, t_im = table[2 * parity], table[2 * parity + 1]
        c_re = c_re + hdot(ht_re[rows], t_re) - hdot(ht_im[rows], t_im)
        c_im = c_im + hdot(ht_re[rows], t_im) + hdot(ht_im[rows], t_re)
    upper = cmul((c_re, c_im), (table[4], table[5]))
    lower = cmul((c_re, c_im), (table[6], table[7]))
    u_ref[0], u_ref[1] = upper
    u_ref[2], u_ref[3] = lower

    @pl.loop(0, OUTER, unroll=4)
    def _(a):
        start = start_ref[a]
        for c in range(chans):
            channel = chan * chans + c
            live = jnp.logical_and(channel >= start, channel < start + ACTIVE).astype(F32)
            lanes = pl.ds(pl.multiple_of(a * LANES, LANES), LANES)
            w_ref[0, c, pl.ds(a, 1), :] = weight_re[c : c + 1, lanes] * live
            w_ref[1, c, pl.ds(a, 1), :] = weight_im[c : c + 1, lanes] * live

    sub_index = lax.broadcasted_iota(jnp.int32, (LANES, LANES), 0)
    lane_index = lax.broadcasted_iota(jnp.int32, (LANES, LANES), 1)
    on_upper = lane_index >= sub_index

    def build_matrix(k):
        def toeplitz(part):
            def rolled(which):
                row = jnp.broadcast_to(u_ref[which, pl.ds(k, 1), :], (LANES, LANES))
                return pltpu.roll(row, 0, 1, stride=1, stride_axis=0)

            return jnp.where(on_upper, rolled(part), rolled(2 + part))

        m_re, m_im = toeplitz(0), toeplitz(1)
        m_ref[k, 0:LANES, 0:LANES] = m_re.astype(BF16)
        m_ref[k, 0:LANES, LANES : 2 * LANES] = m_im.astype(BF16)
        m_ref[k, LANES : 2 * LANES, 0:LANES] = (-m_im).astype(BF16)
        m_ref[k, LANES : 2 * LANES, LANES : 2 * LANES] = m_re.astype(BF16)

    @pl.loop(0, OUTER, unroll=8)
    def _(k):
        build_matrix(k)

    def outer_forward(h):
        first = h * PART_CHUNKS

        @pl.loop(0, PART_CHUNKS)
        def _(r):
            for copy in echo_copies(first + r):
                copy.wait()
            rows = pl.ds(pl.multiple_of((first + r) * ROWS, ROWS), ROWS)
            for c in range(chans):

                def load(a):
                    lanes = slice(a * LANES, (a + 1) * LANES)
                    return (x_re[c, rows, lanes].astype(F32), x_im[c, rows, lanes].astype(F32))

                def store(low, k, value):
                    tmp_re[c, low * 8 + k] = value[0]
                    tmp_im[c, low * 8 + k] = value[1]

                first_pass(load, store, OUTER, 8, -1)
            for c in range(chans):
                out_rows = pl.ds(pl.multiple_of(c * part_rows + r * ROWS, ROWS), ROWS)
                for k in range(8):
                    part = dft(
                        [(tmp_re[c, low * 8 + k], tmp_im[c, low * 8 + k]) for low in range(8)], -1
                    )
                    for j, value in enumerate(part):
                        y_ref[k + 8 * j, out_rows, 0:LANES] = value[0].astype(BF16)
                        y_ref[k + 8 * j, out_rows, LANES : 2 * LANES] = value[1].astype(BF16)

    def filter_inner():
        @pl.loop(0, OUTER, unroll=16)
        def _(k):
            z_ref[k] = jnp.dot(y_ref[k], m_ref[k], preferred_element_type=F32)

    low_half = lax.broadcasted_iota(jnp.int32, (ROWS, LANES), 1) < LANES // 2

    def outer_inverse(i, j):
        for c in range(chans):
            in_rows = pl.ds(pl.multiple_of(c * part_rows + j * ROWS, ROWS), ROWS)

            def load(k):
                return (z_ref[k, in_rows, 0:LANES], z_ref[k, in_rows, LANES : 2 * LANES])

            def store(low, k, value):
                tmp_re[c, low * 8 + k] = value[0]
                tmp_im[c, low * 8 + k] = value[1]

            first_pass(load, store, OUTER, 8, 1)
        for k in range(8):
            total = None
            for c in range(chans):
                part = dft(
                    [(tmp_re[c, low * 8 + k], tmp_im[c, low * 8 + k]) for low in range(8)], 1
                )
                weighted = []
                for j, value in enumerate(part):
                    a = k + 8 * j
                    weight = (w_ref[0, c, a : a + 1, :], w_ref[1, c, a : a + 1, :])
                    weighted.append(cmul(value, weight))
                total = weighted if total is None else [add(o, t) for o, t in zip(total, weighted)]
            for j, (re, im) in enumerate(total):
                half = LANES // 2
                first = jnp.where(low_half, re, pltpu.roll(im, half, 1))
                second = jnp.where(low_half, pltpu.roll(re, half, 1), im)
                for side, value in enumerate((first, second)):
                    owner = 2 * (k + 8 * j) + side
                    to_high, to_core, to_pulse = owner // 64, owner // 32 % 2, owner % 32
                    part_ref[i, to_high, to_core, to_pulse] = value.astype(BF16)

    def sibling_copy(i, to_high):
        return pltpu.make_async_remote_copy(
            src_ref=part_ref.at[i, to_high, 1 - core],
            dst_ref=from_sibling.at[i, to_high],
            send_sem=sib_send.at[i, to_high],
            recv_sem=sib_recv.at[i, to_high],
            device_id=sibling,
            device_id_type=MESH,
        )

    def x_copy(i, n):
        offset = X_OFFSETS[n]
        return pltpu.make_async_remote_copy(
            src_ref=summed.at[i, (x + offset) % 4],
            dst_ref=from_x.at[i, x],
            send_sem=x_send.at[i, n],
            recv_sem=x_recv.at[i, n],
            device_id=along_x(offset),
            device_id_type=MESH,
        )

    def yz_copy(i, n):
        to_y, to_z = along_yz(YZ_OFFSETS[n])
        return pltpu.make_async_remote_copy(
            src_ref=reduced.at[i, to_y * 4 + to_z],
            dst_ref=beam_ref.at[i, mine_yz],
            send_sem=yz_send.at[i, n],
            recv_sem=yz_recv.at[i, n],
            device_id=device_at(x, to_y, to_z, core),
            device_id_type=MESH,
        )

    def own_x_copy(i):
        return pltpu.make_async_copy(summed.at[i, x], from_x.at[i, x], own.at[0, i])

    def own_yz_copy(i):
        return pltpu.make_async_copy(
            reduced.at[i, mine_yz], beam_ref.at[i, mine_yz], own.at[1, i]
        )

    def sum_siblings(i):
        for to_high in range(2):
            sibling_copy(i, to_high).wait_recv()
        for to_x in range(4):

            @pl.loop(0, YZ, unroll=8)
            def _(j):
                block = (to_x % 2) * YZ + j
                total = part_ref[i, to_x // 2, core, block].astype(F32) + from_sibling[
                    i, to_x // 2, block
                ].astype(F32)
                summed[i, to_x, j] = total.astype(BF16)

    def send_along_x(i):
        sum_siblings(i)
        for n in range(len(X_OFFSETS)):
            x_copy(i, n).start()
        own_x_copy(i).start()

    def send_along_yz(i):
        for n in range(len(X_OFFSETS)):
            x_copy(i, n).wait_recv()
        own_x_copy(i).wait()

        @pl.loop(0, YZ, unroll=4)
        def _(j):
            for low in range(2):
                total = from_x[i, low, j].astype(F32) + from_x[i, low + 2, j].astype(F32)
                reduced[i, j, low] = total.astype(BF16)

        for n in range(len(YZ_OFFSETS)):
            yz_copy(i, n).start()
        own_yz_copy(i).start()

    def direct_copy(n):
        to_x, to_y, to_z = anywhere(OFFSETS[n])
        return pltpu.make_async_remote_copy(
            src_ref=summed.at[CHUNKS - 1, to_x, to_y * 4 + to_z],
            dst_ref=last_ref.at[x, mine_yz],
            send_sem=last_send.at[n],
            recv_sem=last_recv.at[n],
            device_id=device_at(to_x, to_y, to_z, core),
            device_id_type=MESH,
        )

    def own_last_copy():
        return pltpu.make_async_copy(
            summed.at[CHUNKS - 1, x, mine_yz], last_ref.at[x, mine_yz], own.at[0, CHUNKS - 1]
        )

    def gains_by_row():
        for copy in gain_copies:
            copy.wait()

        @pl.loop(0, AZ_OUTER, unroll=4)
        def _(j):
            lanes = pl.ds(pl.multiple_of(j * LANES, LANES), LANES)
            q_ref[lanes, :] = jnp.concatenate([g_re[:, lanes], g_im[:, lanes]], axis=0).T

        @pl.loop(0, cols, unroll=8)
        def _(n):
            rate_ref[pl.ds(n, 1), :] = jnp.full((1, LANES), rate[n], F32)

    pieces = 4

    def azimuth_factor(piece):
        each = AZ_OUTER // pieces

        @pl.loop(0, each, unroll=2)
        def _(j):
            k = piece * each + j
            gains = q_ref[pl.ds(k, LANES, stride=AZ_OUTER), :].T
            cosine, sine = unit_of_half_turns(rate_ref[...] * doppler2[pl.ds(k, 1), :])
            re, im = gains[0:cols], gains[cols : 2 * cols]
            factor_re[k] = cosine * re + sine * im
            factor_im[k] = cosine * im - sine * re

    pl.semaphore_wait(barrier, 1 + len(OFFSETS))

    @pl.loop(0, PARTS)
    def _(h):
        outer_forward(h)
        first = h * PART_CHUNKS

        @pl.when(h > 0)
        def _():
            send_along_x(first - 1)

        filter_inner()

        @pl.loop(0, PART_CHUNKS)
        def _(j):
            i = first + j
            outer_inverse(i, j)
            for to_high in range(2):
                sibling_copy(i, to_high).start()

            @pl.when(j > 0)
            def _():
                send_along_x(i - 1)

            @pl.when(i >= 4)
            def _():
                send_along_yz(i - 4)

    gains_by_row()
    sum_siblings(CHUNKS - 1)
    for n in range(len(OFFSETS)):
        direct_copy(n).start()
    own_last_copy().start()

    @pl.loop(0, PART_CHUNKS - 1)
    def _(j):
        send_along_yz(PART_CHUNKS + j)
        azimuth_factor(j)

    azimuth_factor(pieces - 1)

    @pl.loop(0, CHUNKS - 1)
    def _(i):
        for n in range(len(YZ_OFFSETS)):
            yz_copy(i, n).wait()
        own_yz_copy(i).wait()
        for n in range(len(X_OFFSETS)):
            x_copy(i, n).wait_send()

    @pl.loop(0, CHUNKS)
    def _(i):
        for to_high in range(2):
            sibling_copy(i, to_high).wait_send()

    for n in range(len(OFFSETS)):
        direct_copy(n).wait()
    own_last_copy().wait()


def range_call(
    echo_re, echo_im, filter_re, filter_im, weight_re, weight_im, window_start, gain_re, gain_im, rate
):
    chans, pulses, samples = echo_re.shape
    cols = rate.shape[0]
    chunk_rows = ROWS
    vmem = pl.BlockSpec(memory_space=VMEM)
    smem = pl.BlockSpec(memory_space=pltpu.SMEM)
    hbm = pl.BlockSpec(memory_space=pl.ANY)
    dma = pltpu.SemaphoreType.DMA
    factor = VMEM((AZ_OUTER, cols, LANES), F32)
    return pl.pallas_call(
        range_kernel,
        out_shape=(
            VMEM((CHUNKS - 1, YZ, 2, chunk_rows, LANES), BF16),
            VMEM((4, YZ, chunk_rows, LANES), BF16),
            factor,
            factor,
        ),
        in_specs=[vmem, vmem, vmem, vmem, smem, vmem, smem, vmem, hbm, hbm, hbm, hbm],
        out_specs=(vmem, vmem, vmem, vmem),
        scratch_shapes=[
            VMEM((chans, pulses, samples), BF16),
            VMEM((chans, pulses, samples), BF16),
            VMEM((OUTER, chans * PART_CHUNKS * ROWS, 2 * LANES), BF16),
            VMEM((OUTER, chans * PART_CHUNKS * ROWS, 2 * LANES), F32),
            VMEM((OUTER, 2 * LANES, 2 * LANES), BF16),
            VMEM((chans, OUTER, ROWS, LANES), F32),
            VMEM((chans, OUTER, ROWS, LANES), F32),
            VMEM((4, OUTER, LANES), F32),
            VMEM((2, chans, OUTER, LANES), F32),
            VMEM((cols, PULSES), F32),
            VMEM((cols, PULSES), F32),
            VMEM((PULSES, LANES), F32),
            VMEM((cols, LANES), F32),
            VMEM((CHUNKS, 2, 2, AZ_OUTER, chunk_rows, LANES), BF16),
            VMEM((CHUNKS, 2, AZ_OUTER, chunk_rows, LANES), BF16),
            VMEM((CHUNKS, 4, YZ, chunk_rows, LANES), BF16),
            VMEM((CHUNKS, 4, YZ, chunk_rows, LANES), BF16),
            VMEM((CHUNKS, YZ, 2, chunk_rows, LANES), BF16),
            dma((2, CHUNKS)),
            dma((2,)),
            dma((CHUNKS, 2)),
            dma((CHUNKS, 2)),
            dma((CHUNKS, len(X_OFFSETS))),
            dma((CHUNKS, len(X_OFFSETS))),
            dma((CHUNKS, len(YZ_OFFSETS))),
            dma((CHUNKS, len(YZ_OFFSETS))),
            dma((len(OFFSETS),)),
            dma((len(OFFSETS),)),
            dma((2, CHUNKS)),
        ],
        compiler_params=pltpu.CompilerParams(
            collective_id=0, has_side_effects=True, vmem_limit_bytes=54 * MIB
        ),
        name="range_exchange",
    )(
        filter_re.reshape(OUTER, LANES),
        filter_im.reshape(OUTER, LANES),
        weight_re,
        weight_im,
        window_start,
        jnp.asarray(range_tables()),
        rate,
        jnp.asarray(azimuth_tables()[2][2]),
        echo_re,
        echo_im,
        gain_re,
        gain_im,
    )


GROUP = 4


def split_dot(x, table):
    high = x.astype(BF16)
    low = (x - high.astype(F32)).astype(BF16)
    return jnp.dot(
        jnp.concatenate([high, low], axis=1), table, preferred_element_type=F32
    )


def azimuth_kernel(
    beam, last, factor_re, factor_im, forward, inverse, small, eye, out_re, out_im, a_ref, b_ref, tmp_re, tmp_im, o_re, o_im, sems
):
    cols = out_re.shape[0]
    twiddle_re, twiddle_im = small.at[0], small.at[1]

    @pl.loop(0, AZ_OUTER, unroll=16)
    def _(s):
        yz, low = s % YZ, s // YZ
        blocks = [beam[i, yz, low] for i in range(beam.shape[0])]
        blocks.append((last[low, yz].astype(F32) + last[low + 2, yz].astype(F32)).astype(BF16))
        block = jnp.concatenate(blocks, axis=0)
        a_ref[s] = lax.dot_general(
            eye[...], block, (((1,), (1,)), ((), ())), preferred_element_type=F32
        )

    def stash(low, k, value):
        tmp_re[low * 8 + k] = value[0]
        tmp_im[low * 8 + k] = value[1]

    def second(k, sign):
        return dft([(tmp_re[low * 8 + k], tmp_im[low * 8 + k]) for low in range(4)], sign)

    @pl.loop(0, cols // 8)
    def _(r):
        re_rows = pl.ds(pl.multiple_of(r * 8, 8), 8)
        im_rows = pl.ds(pl.multiple_of(cols + r * 8, 8), 8)
        first_pass(lambda s: (a_ref[s, re_rows, :], a_ref[s, im_rows, :]), stash, AZ_OUTER, 4, -1)
        for k in range(8):
            for j, value in enumerate(second(k, -1)):
                at = k + 8 * j
                re, im = cmul(value, (twiddle_re[at : at + 1, :], twiddle_im[at : at + 1, :]))
                b_ref[at, re_rows, 0:LANES] = re
                b_ref[at, re_rows, LANES : 2 * LANES] = im

    @pl.loop(0, AZ_OUTER // GROUP, unroll=8)
    def _(g):
        at = pl.ds(g * GROUP, GROUP)
        x = b_ref[at].reshape(GROUP * cols, 2 * LANES)
        s = split_dot(x, forward[...]).reshape(GROUP, cols, 2 * LANES)
        parts = []
        for i in range(GROUP):
            factor = (factor_re[g * GROUP + i], factor_im[g * GROUP + i])
            re, im = cmul((s[i, :, 0:LANES], s[i, :, LANES : 2 * LANES]), factor)
            parts.append(jnp.concatenate([re, im], axis=1))
        focused = split_dot(jnp.concatenate(parts, axis=0), inverse[...])
        b_ref[at] = focused.reshape(GROUP, cols, 2 * LANES)

    def image_copies(r):
        rows = pl.ds(pl.multiple_of(r * 8, 8), 8)
        return (
            pltpu.make_async_copy(o_re.at[rows], out_re.at[rows], sems.at[0, r]),
            pltpu.make_async_copy(o_im.at[rows], out_im.at[rows], sems.at[1, r]),
        )

    @pl.loop(0, cols // 8)
    def _(r):
        rows = pl.ds(pl.multiple_of(r * 8, 8), 8)

        def load(k):
            value = (b_ref[k, rows, 0:LANES], b_ref[k, rows, LANES : 2 * LANES])
            return cmul(value, (twiddle_re[k : k + 1, :], -twiddle_im[k : k + 1, :]))

        first_pass(load, stash, AZ_OUTER, 4, 1)
        for k in range(8):
            for j, value in enumerate(second(k, 1)):
                s = k + 8 * j
                o_re[rows, s * LANES : (s + 1) * LANES] = value[0]
                o_im[rows, s * LANES : (s + 1) * LANES] = value[1]
        for copy in image_copies(r):
            copy.start()

    @pl.loop(0, cols // 8)
    def _(r):
        for copy in image_copies(r):
            copy.wait()


def azimuth_call(beam, last, factor_re, factor_im):
    cols = factor_re.shape[1]
    forward, inverse, small, eye = azimuth_tables()
    shape = jax.ShapeDtypeStruct((cols, PULSES), F32)
    vmem = pl.BlockSpec(memory_space=VMEM)

    return pl.pallas_call(
        azimuth_kernel,
        out_shape=(shape, shape),
        in_specs=[vmem] * 8,
        out_specs=(pl.BlockSpec(memory_space=pl.ANY),) * 2,
        scratch_shapes=[
            VMEM((AZ_OUTER, 2 * cols, LANES), F32),
            VMEM((AZ_OUTER, cols, 2 * LANES), F32),
            VMEM((AZ_OUTER, 8, LANES), F32),
            VMEM((AZ_OUTER, 8, LANES), F32),
            VMEM((cols, PULSES), F32),
            VMEM((cols, PULSES), F32),
            pltpu.SemaphoreType.DMA((2, cols // 8)),
        ],
        compiler_params=pltpu.CompilerParams(vmem_limit_bytes=32 * MIB),
        name="azimuth_focus",
    )(
        beam,
        last,
        factor_re,
        factor_im,
        jnp.asarray(forward),
        jnp.asarray(inverse),
        jnp.asarray(small),
        jnp.asarray(eye),
    )


def local(
    echo_re,
    echo_im,
    range_filter_re,
    range_filter_im,
    beam_weight_re,
    beam_weight_im,
    window_start,
    azimuth_filter_re,
    azimuth_filter_im,
    migration_rate,
):
    beam, last, factor_re, factor_im = range_call(
        echo_re,
        echo_im,
        range_filter_re,
        range_filter_im,
        beam_weight_re,
        beam_weight_im,
        window_start,
        azimuth_filter_re,
        azimuth_filter_im,
        migration_rate,
    )
    return azimuth_call(beam, last, factor_re, factor_im)


def solution(mesh):
    placed = (
        P("chan", "pulse", None),
        P("chan", "pulse", None),
        P(),
        P(),
        P("chan", None),
        P("chan", None),
        P(),
        P(("chan", "pulse"), None),
        P(("chan", "pulse"), None),
        P(("chan", "pulse")),
    )
    return jax.shard_map(
        local,
        mesh=mesh,
        in_specs=placed,
        out_specs=(P(("chan", "pulse"), None), P(("chan", "pulse"), None)),
        check_vma=False,
    )
```

```python
import functools
import math

import jax
import jax.numpy as jnp
import numpy as np
from jax import lax
from jax.experimental import pallas as pl
from jax.experimental.pallas import tpu as pltpu
from jax.sharding import PartitionSpec as P

ACTIVE = 4
F32 = jnp.float32
BF16 = jnp.bfloat16
MESH = pl.DeviceIdType.MESH
VMEM = pltpu.VMEM
MIB = 1024 * 1024

OUTER = 64
LANES = 128
RANGE = OUTER * LANES
AZ_OUTER = 32
PULSES = AZ_OUTER * LANES


def unit(numerator, denominator):
    angle = 2.0 * np.pi * (np.asarray(numerator) % denominator) / denominator
    return np.cos(angle), np.sin(angle)


def f32_pair(pair):
    return tuple(np.asarray(part, np.float32) for part in pair)


def range_tables():
    row = np.arange(OUTER)[:, None]
    lane = np.arange(LANES)[None, :]
    tables = []
    for parity in (0, 1):
        re, im = unit(lane * (2 * row + parity), LANES)
        tables += f32_pair((re / RANGE, im / RANGE))
    tables += f32_pair(unit(row * lane, RANGE))
    tables += f32_pair(unit(row * (lane - LANES), RANGE))
    return np.stack(tables)


def real_form(pair):
    re, im = pair
    return np.block([[re, im], [-im, re]])


def split_table(table):
    high = table.astype(BF16)
    return np.concatenate([high, high], axis=0)


def azimuth_tables():
    index = np.arange(LANES)
    row = np.arange(AZ_OUTER)[:, None]
    lane = index[None, :]
    grid = index[:, None] * index[None, :]
    forward = split_table(real_form(unit(-grid, LANES)))
    inverse = split_table(real_form(unit(grid, LANES)) / PULSES)
    twiddle_re, twiddle_im = unit(-row * lane, PULSES)
    frequency = row + AZ_OUTER * lane
    doppler = ((frequency + PULSES // 2) % PULSES - PULSES // 2) * (2.0 / PULSES)
    small = np.stack(f32_pair((twiddle_re, twiddle_im)) + (np.asarray(doppler**2, np.float32),))
    eye = np.eye(LANES).astype(BF16)
    return forward, inverse, small, eye


def times(value, numerator, denominator):
    re, im = value
    eighth = (numerator * 8) / denominator % 8
    if eighth == 0:
        return value
    if eighth == 2:
        return (-im, re)
    if eighth == 4:
        return (-re, -im)
    if eighth == 6:
        return (im, -re)
    half = math.sqrt(0.5)
    if eighth == 1:
        return ((re - im) * half, (re + im) * half)
    if eighth == 3:
        return ((re + im) * -half, (re - im) * half)
    if eighth == 5:
        return ((im - re) * half, (re + im) * -half)
    if eighth == 7:
        return ((re + im) * half, (im - re) * half)
    cosine = math.cos(2.0 * math.pi * numerator / denominator)
    sine = math.sin(2.0 * math.pi * numerator / denominator)
    return (re * cosine - im * sine, re * sine + im * cosine)


def add(one, two):
    return (one[0] + two[0], one[1] + two[1])


def sub(one, two):
    return (one[0] - two[0], one[1] - two[1])


def dft(values, sign):
    count = len(values)
    if count == 1:
        return values
    even = dft(values[0::2], sign)
    odd = dft(values[1::2], sign)
    odd = [times(value, sign * k, count) for k, value in enumerate(odd)]
    return [add(e, o) for e, o in zip(even, odd)] + [sub(e, o) for e, o in zip(even, odd)]


def cmul(one, two):
    return (one[0] * two[0] - one[1] * two[1], one[0] * two[1] + one[1] * two[0])


def first_pass(load, store, count, fine, sign):
    high = count // fine
    for low in range(fine):
        part = dft([load(fine * j + low) for j in range(high)], sign)
        for k, value in enumerate(part):
            store(low, k, times(value, sign * low * k, count))


def unit_of_half_turns(turns):
    quarter = jnp.floor(turns * 2.0 + 0.5)
    x = (turns - quarter * 0.5) * math.pi
    y = x * x
    sine = x * (1.0 + y * (-1.0 / 6 + y * (1.0 / 120 + y * (-1.0 / 5040 + y * (1.0 / 362880)))))
    cosine = 1.0 + y * (-0.5 + y * (1.0 / 24 + y * (-1.0 / 720 + y * (1.0 / 40320))))
    index = quarter.astype(jnp.int32)
    swap = index % 2 == 1
    one = jnp.where(swap, sine, cosine)
    two = jnp.where(swap, cosine, sine)
    one = jnp.where((index + 1) // 2 % 2 == 1, -one, one)
    two = jnp.where(index // 2 % 2 == 1, -two, two)
    return one, two


ROWS = 16
CHUNKS = 8
PARTS = 2
PART_CHUNKS = CHUNKS // PARTS
X_OFFSETS = (2, 1, 3)
YZ_OFFSETS = sorted(
    [(y, z) for y in range(4) for z in range(4) if (y, z) != (0, 0)],
    key=lambda offset: -sum(min(d, 4 - d) for d in offset),
)
YZ = 16
OFFSETS = sorted(
    [(x, y, z) for x in range(4) for y in range(4) for z in range(4) if (x, y, z) != (0, 0, 0)],
    key=lambda offset: -sum(min(d, 4 - d) for d in offset),
)


def place():
    chan, pulse = lax.axis_index("chan"), lax.axis_index("pulse")
    return (chan // 2) * 2 + pulse // 16, (pulse // 4) % 4, pulse % 4, chan % 2


def device_at(x, y, z, core):
    return ((x // 2) * 2 + core, (x % 2) * 16 + y * 4 + z)


def range_kernel(
    filter_re,
    filter_im,
    weight_re,
    weight_im,
    start_ref,
    table,
    rate,
    doppler2,
    echo_re,
    echo_im,
    gain_re,
    gain_im,
    beam_ref,
    last_ref,
    factor_re,
    factor_im,
    x_re,
    x_im,
    y_ref,
    z_ref,
    m_ref,
    tmp_re,
    tmp_im,
    u_ref,
    w_ref,
    g_re,
    g_im,
    q_ref,
    rate_ref,
    part_ref,
    from_sibling,
    summed,
    from_x,
    reduced,
    echo_sems,
    gain_sems,
    sib_send,
    sib_recv,
    x_send,
    x_recv,
    yz_send,
    yz_recv,
    last_send,
    last_recv,
    own,
):
    chans, pulses = echo_re.shape[0], echo_re.shape[1]
    part_rows = PART_CHUNKS * ROWS
    cols = rate.shape[0]
    chan = lax.axis_index("chan")
    x, y, z, core = place()
    mine_yz = y * 4 + z
    sibling = device_at(x, y, z, 1 - core)

    def along_x(offset):
        return device_at((x + offset) % 4, y, z, core)

    def along_yz(offset):
        return (y + offset[0]) % 4, (z + offset[1]) % 4

    def anywhere(offset):
        return (x + offset[0]) % 4, (y + offset[1]) % 4, (z + offset[2]) % 4

    def echo_copies(i):
        rows = pl.ds(pl.multiple_of(i * ROWS, ROWS), ROWS)
        return (
            pltpu.make_async_copy(echo_re.at[:, rows], x_re.at[:, rows], echo_sems.at[0, i]),
            pltpu.make_async_copy(echo_im.at[:, rows], x_im.at[:, rows], echo_sems.at[1, i]),
        )

    @pl.loop(0, CHUNKS)
    def _(i):
        for copy in echo_copies(i):
            copy.start()

    gain_copies = (
        pltpu.make_async_copy(gain_re, g_re, gain_sems.at[0]),
        pltpu.make_async_copy(gain_im, g_im, gain_sems.at[1]),
    )
    for copy in gain_copies:
        copy.start()

    barrier = pltpu.get_barrier_semaphore()
    pl.semaphore_signal(barrier, inc=1, device_id=sibling, device_id_type=MESH)
    for offset in OFFSETS:
        pl.semaphore_signal(
            barrier, inc=1, device_id=device_at(*anywhere(offset), core), device_id_type=MESH
        )

    def hdot(one, two):
        return jnp.dot(one, two, precision=lax.Precision.HIGHEST, preferred_element_type=F32)

    ht_re, ht_im = filter_re[...].T, filter_im[...].T
    c_re = jnp.zeros((OUTER, LANES), F32)
    c_im = jnp.zeros((OUTER, LANES), F32)
    for parity in (0, 1):
        rows = slice(parity * OUTER, (parity + 1) * OUTER)
        t_re, t_im = table[2 * parity], table[2 * parity + 1]
        c_re = c_re + hdot(ht_re[rows], t_re) - hdot(ht_im[rows], t_im)
        c_im = c_im + hdot(ht_re[rows], t_im) + hdot(ht_im[rows], t_re)
    upper = cmul((c_re, c_im), (table[4], table[5]))
    lower = cmul((c_re, c_im), (table[6], table[7]))
    u_ref[0], u_ref[1] = upper
    u_ref[2], u_ref[3] = lower

    @pl.loop(0, OUTER, unroll=16)
    def _(a):
        start = start_ref[a]
        for c in range(chans):
            channel = chan * chans + c
            live = jnp.logical_and(channel >= start, channel < start + ACTIVE).astype(F32)
            lanes = pl.ds(pl.multiple_of(a * LANES, LANES), LANES)
            w_ref[0, c, pl.ds(a, 1), :] = weight_re[c : c + 1, lanes] * live
            w_ref[1, c, pl.ds(a, 1), :] = weight_im[c : c + 1, lanes] * live

    sub_index = lax.broadcasted_iota(jnp.int32, (LANES, LANES), 0)
    lane_index = lax.broadcasted_iota(jnp.int32, (LANES, LANES), 1)
    on_upper = lane_index >= sub_index

    def build_matrix(k):
        def toeplitz(part):
            def rolled(which):
                row = jnp.broadcast_to(u_ref[which, pl.ds(k, 1), :], (LANES, LANES))
                return pltpu.roll(row, 0, 1, stride=1, stride_axis=0)

            return jnp.where(on_upper, rolled(part), rolled(2 + part))

        m_re, m_im = toeplitz(0), toeplitz(1)
        m_ref[k, 0:LANES, 0:LANES] = m_re.astype(BF16)
        m_ref[k, 0:LANES, LANES : 2 * LANES] = m_im.astype(BF16)
        m_ref[k, LANES : 2 * LANES, 0:LANES] = (-m_im).astype(BF16)
        m_ref[k, LANES : 2 * LANES, LANES : 2 * LANES] = m_re.astype(BF16)

    @pl.loop(0, OUTER, unroll=16)
    def _(k):
        build_matrix(k)

    def outer_forward(h):
        first = h * PART_CHUNKS

        @pl.loop(0, PART_CHUNKS)
        def _(r):
            for copy in echo_copies(first + r):
                copy.wait()
            rows = pl.ds(pl.multiple_of((first + r) * ROWS, ROWS), ROWS)
            for c in range(chans):

                def load(a):
                    lanes = slice(a * LANES, (a + 1) * LANES)
                    return (x_re[c, rows, lanes].astype(F32), x_im[c, rows, lanes].astype(F32))

                def store(low, k, value):
                    tmp_re[c, low * 8 + k] = value[0]
                    tmp_im[c, low * 8 + k] = value[1]

                first_pass(load, store, OUTER, 8, -1)
            for c in range(chans):
                out_rows = pl.ds(pl.multiple_of(c * part_rows + r * ROWS, ROWS), ROWS)
                for k in range(8):
                    part = dft(
                        [(tmp_re[c, low * 8 + k], tmp_im[c, low * 8 + k]) for low in range(8)], -1
                    )
                    for j, value in enumerate(part):
                        y_ref[k + 8 * j, out_rows, 0:LANES] = value[0].astype(BF16)
                        y_ref[k + 8 * j, out_rows, LANES : 2 * LANES] = value[1].astype(BF16)

    def filter_inner():
        @pl.loop(0, OUTER, unroll=16)
        def _(k):
            z_ref[k] = jnp.dot(y_ref[k], m_ref[k], preferred_element_type=F32)

    low_half = lax.broadcasted_iota(jnp.int32, (ROWS, LANES), 1) < LANES // 2

    def outer_inverse(i, j):
        for c in range(chans):
            in_rows = pl.ds(pl.multiple_of(c * part_rows + j * ROWS, ROWS), ROWS)

            def load(k):
                return (z_ref[k, in_rows, 0:LANES], z_ref[k, in_rows, LANES : 2 * LANES])

            def store(low, k, value):
                tmp_re[c, low * 8 + k] = value[0]
                tmp_im[c, low * 8 + k] = value[1]

            first_pass(load, store, OUTER, 8, 1)
        for k in range(8):
            total = None
            for c in range(chans):
                part = dft(
                    [(tmp_re[c, low * 8 + k], tmp_im[c, low * 8 + k]) for low in range(8)], 1
                )
                weighted = []
                for j, value in enumerate(part):
                    a = k + 8 * j
                    weight = (w_ref[0, c, a : a + 1, :], w_ref[1, c, a : a + 1, :])
                    weighted.append(cmul(value, weight))
                total = weighted if total is None else [add(o, t) for o, t in zip(total, weighted)]
            for j, (re, im) in enumerate(total):
                half = LANES // 2
                first = jnp.where(low_half, re, pltpu.roll(im, half, 1))
                second = jnp.where(low_half, pltpu.roll(re, half, 1), im)
                for side, value in enumerate((first, second)):
                    owner = 2 * (k + 8 * j) + side
                    to_high, to_core, to_pulse = owner // 64, owner // 32 % 2, owner % 32
                    part_ref[i, to_high, to_core, to_pulse] = value.astype(BF16)

    def sibling_copy(i, to_high):
        return pltpu.make_async_remote_copy(
            src_ref=part_ref.at[i, to_high, 1 - core],
            dst_ref=from_sibling.at[i, to_high],
            send_sem=sib_send.at[i, to_high],
            recv_sem=sib_recv.at[i, to_high],
            device_id=sibling,
            device_id_type=MESH,
        )

    def x_copy(i, n):
        offset = X_OFFSETS[n]
        return pltpu.make_async_remote_copy(
            src_ref=summed.at[i, (x + offset) % 4],
            dst_ref=from_x.at[i, x],
            send_sem=x_send.at[i, n],
            recv_sem=x_recv.at[i, n],
            device_id=along_x(offset),
            device_id_type=MESH,
        )

    def yz_copy(i, n):
        to_y, to_z = along_yz(YZ_OFFSETS[n])
        return pltpu.make_async_remote_copy(
            src_ref=reduced.at[i, to_y * 4 + to_z],
            dst_ref=beam_ref.at[i, mine_yz],
            send_sem=yz_send.at[i, n],
            recv_sem=yz_recv.at[i, n],
            device_id=device_at(x, to_y, to_z, core),
            device_id_type=MESH,
        )

    def own_x_copy(i):
        return pltpu.make_async_copy(summed.at[i, x], from_x.at[i, x], own.at[0, i])

    def own_yz_copy(i):
        return pltpu.make_async_copy(
            reduced.at[i, mine_yz], beam_ref.at[i, mine_yz], own.at[1, i]
        )

    def sum_siblings(i):
        for to_high in range(2):
            sibling_copy(i, to_high).wait_recv()
        for to_x in range(4):

            @pl.loop(0, YZ, unroll=8)
            def _(j):
                block = (to_x % 2) * YZ + j
                total = part_ref[i, to_x // 2, core, block].astype(F32) + from_sibling[
                    i, to_x // 2, block
                ].astype(F32)
                summed[i, to_x, j] = total.astype(BF16)

    def send_along_x(i):
        sum_siblings(i)
        for n in range(len(X_OFFSETS)):
            x_copy(i, n).start()
        own_x_copy(i).start()

    def send_along_yz(i):
        for n in range(len(X_OFFSETS)):
            x_copy(i, n).wait_recv()
        own_x_copy(i).wait()

        @pl.loop(0, YZ, unroll=4)
        def _(j):
            for low in range(2):
                total = from_x[i, low, j].astype(F32) + from_x[i, low + 2, j].astype(F32)
                reduced[i, j, low] = total.astype(BF16)

        for n in range(len(YZ_OFFSETS)):
            yz_copy(i, n).start()
        own_yz_copy(i).start()

    def direct_copy(n):
        to_x, to_y, to_z = anywhere(OFFSETS[n])
        return pltpu.make_async_remote_copy(
            src_ref=summed.at[CHUNKS - 1, to_x, to_y * 4 + to_z],
            dst_ref=last_ref.at[x, mine_yz],
            send_sem=last_send.at[n],
            recv_sem=last_recv.at[n],
            device_id=device_at(to_x, to_y, to_z, core),
            device_id_type=MESH,
        )

    def own_last_copy():
        return pltpu.make_async_copy(
            summed.at[CHUNKS - 1, x, mine_yz], last_ref.at[x, mine_yz], own.at[0, CHUNKS - 1]
        )

    def gains_by_row():
        for copy in gain_copies:
            copy.wait()

        @pl.loop(0, AZ_OUTER, unroll=4)
        def _(j):
            lanes = pl.ds(pl.multiple_of(j * LANES, LANES), LANES)
            q_ref[lanes, :] = jnp.concatenate([g_re[:, lanes], g_im[:, lanes]], axis=0).T

        @pl.loop(0, cols, unroll=8)
        def _(n):
            rate_ref[pl.ds(n, 1), :] = jnp.full((1, LANES), rate[n], F32)

    pieces = 4

    def azimuth_factor(piece):
        each = AZ_OUTER // pieces

        @pl.loop(0, each, unroll=2)
        def _(j):
            k = piece * each + j
            gains = q_ref[pl.ds(k, LANES, stride=AZ_OUTER), :].T
            cosine, sine = unit_of_half_turns(rate_ref[...] * doppler2[pl.ds(k, 1), :])
            re, im = gains[0:cols], gains[cols : 2 * cols]
            factor_re[k] = cosine * re + sine * im
            factor_im[k] = cosine * im - sine * re

    pl.semaphore_wait(barrier, 1 + len(OFFSETS))

    @pl.loop(0, PARTS)
    def _(h):
        outer_forward(h)
        first = h * PART_CHUNKS

        @pl.when(h > 0)
        def _():
            send_along_x(first - 1)

        filter_inner()

        @pl.loop(0, PART_CHUNKS)
        def _(j):
            i = first + j
            outer_inverse(i, j)
            for to_high in range(2):
                sibling_copy(i, to_high).start()

            @pl.when(j > 0)
            def _():
                send_along_x(i - 1)

            @pl.when(i >= 4)
            def _():
                send_along_yz(i - 4)

    gains_by_row()
    sum_siblings(CHUNKS - 1)
    for n in range(len(OFFSETS)):
        direct_copy(n).start()
    own_last_copy().start()

    @pl.loop(0, PART_CHUNKS - 1)
    def _(j):
        send_along_yz(PART_CHUNKS + j)
        azimuth_factor(j)

    azimuth_factor(pieces - 1)

    @pl.loop(0, CHUNKS - 1)
    def _(i):
        for n in range(len(YZ_OFFSETS)):
            yz_copy(i, n).wait()
        own_yz_copy(i).wait()
        for n in range(len(X_OFFSETS)):
            x_copy(i, n).wait_send()

    @pl.loop(0, CHUNKS)
    def _(i):
        for to_high in range(2):
            sibling_copy(i, to_high).wait_send()

    for n in range(len(OFFSETS)):
        direct_copy(n).wait()
    own_last_copy().wait()


def range_call(
    echo_re, echo_im, filter_re, filter_im, weight_re, weight_im, window_start, gain_re, gain_im, rate
):
    chans, pulses, samples = echo_re.shape
    cols = rate.shape[0]
    chunk_rows = ROWS
    vmem = pl.BlockSpec(memory_space=VMEM)
    smem = pl.BlockSpec(memory_space=pltpu.SMEM)
    hbm = pl.BlockSpec(memory_space=pl.ANY)
    dma = pltpu.SemaphoreType.DMA
    factor = VMEM((AZ_OUTER, cols, LANES), F32)
    return pl.pallas_call(
        range_kernel,
        out_shape=(
            VMEM((CHUNKS - 1, YZ, 2, chunk_rows, LANES), BF16),
            VMEM((4, YZ, chunk_rows, LANES), BF16),
            factor,
            factor,
        ),
        in_specs=[vmem, vmem, vmem, vmem, smem, vmem, smem, vmem, hbm, hbm, hbm, hbm],
        out_specs=(vmem, vmem, vmem, vmem),
        scratch_shapes=[
            VMEM((chans, pulses, samples), BF16),
            VMEM((chans, pulses, samples), BF16),
            VMEM((OUTER, chans * PART_CHUNKS * ROWS, 2 * LANES), BF16),
            VMEM((OUTER, chans * PART_CHUNKS * ROWS, 2 * LANES), F32),
            VMEM((OUTER, 2 * LANES, 2 * LANES), BF16),
            VMEM((chans, OUTER, ROWS, LANES), F32),
            VMEM((chans, OUTER, ROWS, LANES), F32),
            VMEM((4, OUTER, LANES), F32),
            VMEM((2, chans, OUTER, LANES), F32),
            VMEM((cols, PULSES), F32),
            VMEM((cols, PULSES), F32),
            VMEM((PULSES, LANES), F32),
            VMEM((cols, LANES), F32),
            VMEM((CHUNKS, 2, 2, AZ_OUTER, chunk_rows, LANES), BF16),
            VMEM((CHUNKS, 2, AZ_OUTER, chunk_rows, LANES), BF16),
            VMEM((CHUNKS, 4, YZ, chunk_rows, LANES), BF16),
            VMEM((CHUNKS, 4, YZ, chunk_rows, LANES), BF16),
            VMEM((CHUNKS, YZ, 2, chunk_rows, LANES), BF16),
            dma((2, CHUNKS)),
            dma((2,)),
            dma((CHUNKS, 2)),
            dma((CHUNKS, 2)),
            dma((CHUNKS, len(X_OFFSETS))),
            dma((CHUNKS, len(X_OFFSETS))),
            dma((CHUNKS, len(YZ_OFFSETS))),
            dma((CHUNKS, len(YZ_OFFSETS))),
            dma((len(OFFSETS),)),
            dma((len(OFFSETS),)),
            dma((2, CHUNKS)),
        ],
        compiler_params=pltpu.CompilerParams(
            collective_id=0, has_side_effects=True, vmem_limit_bytes=54 * MIB
        ),
        name="range_exchange",
    )(
        filter_re.reshape(OUTER, LANES),
        filter_im.reshape(OUTER, LANES),
        weight_re,
        weight_im,
        window_start,
        jnp.asarray(range_tables()),
        rate,
        jnp.asarray(azimuth_tables()[2][2]),
        echo_re,
        echo_im,
        gain_re,
        gain_im,
    )


GROUP = 4


def split_dot(x, table):
    high = x.astype(BF16)
    low = (x - high.astype(F32)).astype(BF16)
    return jnp.dot(
        jnp.concatenate([high, low], axis=1), table, preferred_element_type=F32
    )


def azimuth_kernel(
    beam, last, factor_re, factor_im, forward, inverse, small, eye, out_re, out_im, a_ref, b_ref, tmp_re, tmp_im, o_re, o_im, sems
):
    cols = out_re.shape[0]
    twiddle_re, twiddle_im = small.at[0], small.at[1]

    @pl.loop(0, AZ_OUTER, unroll=16)
    def _(s):
        yz, low = s % YZ, s // YZ
        blocks = [beam[i, yz, low] for i in range(beam.shape[0])]
        blocks.append((last[low, yz].astype(F32) + last[low + 2, yz].astype(F32)).astype(BF16))
        block = jnp.concatenate(blocks, axis=0)
        a_ref[s] = lax.dot_general(
            eye[...], block, (((1,), (1,)), ((), ())), preferred_element_type=F32
        )

    def stash(low, k, value):
        tmp_re[low * 8 + k] = value[0]
        tmp_im[low * 8 + k] = value[1]

    def second(k, sign):
        return dft([(tmp_re[low * 8 + k], tmp_im[low * 8 + k]) for low in range(4)], sign)

    @pl.loop(0, cols // 8)
    def _(r):
        re_rows = pl.ds(pl.multiple_of(r * 8, 8), 8)
        im_rows = pl.ds(pl.multiple_of(cols + r * 8, 8), 8)
        first_pass(lambda s: (a_ref[s, re_rows, :], a_ref[s, im_rows, :]), stash, AZ_OUTER, 4, -1)
        for k in range(8):
            for j, value in enumerate(second(k, -1)):
                at = k + 8 * j
                re, im = cmul(value, (twiddle_re[at : at + 1, :], twiddle_im[at : at + 1, :]))
                b_ref[at, re_rows, 0:LANES] = re
                b_ref[at, re_rows, LANES : 2 * LANES] = im

    @pl.loop(0, AZ_OUTER // GROUP, unroll=8)
    def _(g):
        at = pl.ds(g * GROUP, GROUP)
        x = b_ref[at].reshape(GROUP * cols, 2 * LANES)
        s = split_dot(x, forward[...]).reshape(GROUP, cols, 2 * LANES)
        parts = []
        for i in range(GROUP):
            factor = (factor_re[g * GROUP + i], factor_im[g * GROUP + i])
            re, im = cmul((s[i, :, 0:LANES], s[i, :, LANES : 2 * LANES]), factor)
            parts.append(jnp.concatenate([re, im], axis=1))
        focused = split_dot(jnp.concatenate(parts, axis=0), inverse[...])
        b_ref[at] = focused.reshape(GROUP, cols, 2 * LANES)

    def image_copies(r):
        rows = pl.ds(pl.multiple_of(r * 8, 8), 8)
        return (
            pltpu.make_async_copy(o_re.at[rows], out_re.at[rows], sems.at[0, r]),
            pltpu.make_async_copy(o_im.at[rows], out_im.at[rows], sems.at[1, r]),
        )

    @pl.loop(0, cols // 8)
    def _(r):
        rows = pl.ds(pl.multiple_of(r * 8, 8), 8)

        def load(k):
            value = (b_ref[k, rows, 0:LANES], b_ref[k, rows, LANES : 2 * LANES])
            return cmul(value, (twiddle_re[k : k + 1, :], -twiddle_im[k : k + 1, :]))

        first_pass(load, stash, AZ_OUTER, 4, 1)
        for k in range(8):
            for j, value in enumerate(second(k, 1)):
                s = k + 8 * j
                o_re[rows, s * LANES : (s + 1) * LANES] = value[0]
                o_im[rows, s * LANES : (s + 1) * LANES] = value[1]
        for copy in image_copies(r):
            copy.start()

    @pl.loop(0, cols // 8)
    def _(r):
        for copy in image_copies(r):
            copy.wait()


def azimuth_call(beam, last, factor_re, factor_im):
    cols = factor_re.shape[1]
    forward, inverse, small, eye = azimuth_tables()
    shape = jax.ShapeDtypeStruct((cols, PULSES), F32)
    vmem = pl.BlockSpec(memory_space=VMEM)

    return pl.pallas_call(
        azimuth_kernel,
        out_shape=(shape, shape),
        in_specs=[vmem] * 8,
        out_specs=(pl.BlockSpec(memory_space=pl.ANY),) * 2,
        scratch_shapes=[
            VMEM((AZ_OUTER, 2 * cols, LANES), F32),
            VMEM((AZ_OUTER, cols, 2 * LANES), F32),
            VMEM((AZ_OUTER, 8, LANES), F32),
            VMEM((AZ_OUTER, 8, LANES), F32),
            VMEM((cols, PULSES), F32),
            VMEM((cols, PULSES), F32),
            pltpu.SemaphoreType.DMA((2, cols // 8)),
        ],
        compiler_params=pltpu.CompilerParams(vmem_limit_bytes=32 * MIB),
        name="azimuth_focus",
    )(
        beam,
        last,
        factor_re,
        factor_im,
        jnp.asarray(forward),
        jnp.asarray(inverse),
        jnp.asarray(small),
        jnp.asarray(eye),
    )


def local(
    echo_re,
    echo_im,
    range_filter_re,
    range_filter_im,
    beam_weight_re,
    beam_weight_im,
    window_start,
    azimuth_filter_re,
    azimuth_filter_im,
    migration_rate,
):
    beam, last, factor_re, factor_im = range_call(
        echo_re,
        echo_im,
        range_filter_re,
        range_filter_im,
        beam_weight_re,
        beam_weight_im,
        window_start,
        azimuth_filter_re,
        azimuth_filter_im,
        migration_rate,
    )
    return azimuth_call(beam, last, factor_re, factor_im)


def solution(mesh):
    placed = (
        P("chan", "pulse", None),
        P("chan", "pulse", None),
        P(),
        P(),
        P("chan", None),
        P("chan", None),
        P(),
        P(("chan", "pulse"), None),
        P(("chan", "pulse"), None),
        P(("chan", "pulse")),
    )
    return jax.shard_map(
        local,
        mesh=mesh,
        in_specs=placed,
        out_specs=(P(("chan", "pulse"), None), P(("chan", "pulse"), None)),
        check_vma=False,
    )
```
